32 devices in a mesh: prow: 8 (over z, y), pcol: 4 (over x, core).
Axes of the slice: x: 2, y: 2, z: 4, core: 2. Of those that a mesh axis runs over, the one named last changes fastest.
Arguments:
- front: float32 [8, 8, 16, 4, 128, 128], P(None, 'prow', None, 'pcol'), may hold values from -6 to 6, as said below
- child_blocks: float32 [1024, 128, 128], P(('prow', 'pcol')), may hold values from -3 to 3
- owners: int32 [1024, 1], P(('prow', 'pcol')), may hold values from 0 to 31; in each aligned block of 32 rows (0 to 31, 32 to 63, ...) at most 2 rows name the same one
- slots: int32 [1024], P(('prow', 'pcol')), may hold values from 1 to 127
- pattern: int32 [2, 64], replicated, may hold values 0 or 1
Outputs:
- factored: float32 [8, 8, 16, 4, 128, 128], P(None, 'prow', None, 'pcol')
The draws below stay inside these ranges and needn't reach their ends.
Inputs may be any that keep to these rules, and one draw needn't show every extreme that they name: `front`: in the leading 2 * 256 rows and columns, off-diagonal entries lie within 2 / 512 in magnitude and diagonal entries within 3 to 5. `owners`: among the 32 child blocks of one device no owner is named more than 2 times; some owner is named exactly 2 times. `slots`: slot 0 never occurs.
All inputs are finite; a program needn't handle non-finite values.
Results may differ from the reference program's by a relative error of at most 0.0001.
Values sent between devices are 32-bit elements; how exact they have to be, the bound alone decides.
No kernel may reach another device: no remote copies, remote signals or barrier semaphores. Data moves between devices by JAX's collectives and lax.ppermute only.
A program may use at most 192 MiB of HBM per device.

```python
import math
import jax
import jax.numpy as jnp
import numpy as np
from jax import lax

TILE = 128
PANEL = 256
CAP = 2
BR = 8
PROWS = 8
PCOLS = 4
NB = 64
BC = 16
CHILDREN = 32
CHILD_ALL = 1024
DEVICES = 32


def draw_front(key, part):
    key_off, key_diag, key_rest = jax.random.split(key, 3)
    shape = (BR, PROWS, BC, PCOLS, TILE, TILE)
    row_block = lax.broadcasted_iota(jnp.int32, shape, 0) * PROWS + lax.broadcasted_iota(jnp.int32, shape, 1)
    col_block = lax.broadcasted_iota(jnp.int32, shape, 2) * PCOLS + lax.broadcasted_iota(jnp.int32, shape, 3)
    glob_row = row_block * TILE + lax.broadcasted_iota(jnp.int32, shape, 4)
    glob_col = col_block * TILE + lax.broadcasted_iota(jnp.int32, shape, 5)
    lead = 2 * PANEL
    leading = (glob_row < lead) & (glob_col < lead)
    off_part = jax.random.uniform(key_off, shape, jnp.float32, -1.0, 1.0) * (2.0 / lead)
    diag_part = jax.random.uniform(key_diag, shape, jnp.float32, 3.0, 5.0)
    rest = jnp.clip(jax.random.normal(key_rest, shape, jnp.float32), -5.5, 5.5)
    rest = rest * jnp.where(glob_col < lead, 0.5, 1.0)
    inner = jnp.where(glob_row == glob_col, diag_part, off_part)
    return jnp.where(leading, inner, rest).astype(jnp.float32)


def with_ends(values, key, low, largest):
    index_at = [jax.random.randint(jax.random.fold_in(key, axis), (), 0, length) for axis, length in enumerate(values.shape)]
    main_axis = values.shape.index(max(values.shape))
    neighbour = index_at[:main_axis] + [(index_at[main_axis] + 1) % values.shape[main_axis]] + index_at[main_axis + 1:]
    return values.at[tuple(index_at)].set(low).at[tuple(neighbour)].set(largest)


def block_levels(stream_key, dims, shards, low, largest):
    loudness = 1.0
    for dim, parts in shards:
        steps = jax.random.uniform(jax.random.fold_in(jax.random.fold_in(stream_key, 6), dim), (parts,), jnp.float32, low / len(shards), largest / len(shards))
        loudness = loudness * jnp.repeat(jnp.exp(steps), dims[dim] // parts).reshape((-1,) + (1,) * (len(dims) - 1 - dim))
    return loudness


def assign_block(stream_key, own, number, rows, amount, top, bound, slope):
    ranking = jax.random.permutation(stream_key, amount)
    heavy_load, ordinary = shares(amount, rows * top, bound, slope, True), shares(amount, rows * top, bound, slope, False)
    places = jnp.arange(amount)

    def named(tallies, offset_by):
        used = int((tallies > 0).sum())
        fixed = max(1, used // 4)
        passed = fixed + (places - fixed + offset_by * (used - fixed)) % max(1, amount - fixed)
        return jnp.zeros((amount,), jnp.int32).at[ranking[jnp.where(places < fixed, places, passed)]].set(jnp.asarray(tallies, jnp.int32))

    tallies = jnp.where(number % 4 == 0, named(heavy_load, number // 4), named(ordinary, number - number // 4 - 1))
    mixed = jax.random.permutation(jax.random.fold_in(own, 3), amount)
    donor, taker = mixed[0:amount // 2 * 2:2], mixed[1:amount // 2 * 2:2]
    slack = jnp.minimum(tallies[donor] - 1, bound - tallies[taker]) // 2
    slack = jnp.where((donor == ranking[0]) | (taker == ranking[0]) | (tallies[taker] == 0), 0, jnp.maximum(slack, 0))
    passed = jax.random.randint(jax.random.fold_in(own, 4), (amount // 2,), 0, 1 << 20) % (slack + 1)
    tallies = tallies.at[donor].add(-passed).at[taker].add(passed)
    items = jnp.searchsorted(jnp.cumsum(tallies), jnp.arange(rows * top), side="right").astype(jnp.int32)
    grid = items.reshape(top, rows).T
    grid = grid[jax.random.permutation(jax.random.fold_in(own, 1), rows)]
    offset_by = jax.random.randint(jax.random.fold_in(own, 2), (rows, 1), 0, top)
    return jnp.take_along_axis(grid, (jnp.arange(top)[None, :] + offset_by) % top, axis=1)


def shares(number_of, total, limit, skew, full):
    weights = [(1 << 20) // math.isqrt(rank ** skew) + 1 for rank in range(1, number_of + 1)]
    largest = limit if full else min(limit, max(-(-total // number_of), total * weights[0] // sum(weights)))
    least = 1 if total - largest >= number_of - 1 else 0
    holding, surplus = [largest] + [least] * (number_of - 1), total - largest - least * (number_of - 1)
    while surplus > 0:
        movable = [i for i in range(1, number_of) if holding[i] < largest] or [i for i in range(1, number_of) if holding[i] < limit]
        mass, budget = sum([weights[i] for i in movable]), surplus
        for i in movable:
            addition = min(limit - holding[i], max(1, budget * weights[i] // mass), surplus)
            holding[i] = holding[i] + addition
            surplus = surplus - addition
    return np.array(holding)


def normal_values(stream_key, extent, deviation, bound, cuts=(), held_as=jnp.bfloat16):
    values = jax.random.normal(stream_key, extent, jnp.float32) * deviation
    if len(cuts) > 0:
        values = block_levels(stream_key, extent, cuts, -0.22, 0.18) * values
    return jnp.clip(values, min=-bound, max=bound).astype(held_as)


def setup_inputs(seed: int = 0) -> dict:
    arg_keys = jax.random.split(jax.random.key(seed), 6)
    front = draw_front(jax.random.fold_in(arg_keys[5], 71), 0)
    child_blocks = normal_values(arg_keys[1], (CHILD_ALL, TILE, TILE), 0.5, 3.0, ((0, 32),), jnp.float32)
    owners_keys = jax.random.split(jax.random.fold_in(arg_keys[2], 1), CHILD_ALL // CHILDREN)
    owners_turns = jax.random.permutation(jax.random.fold_in(arg_keys[2], 3), CHILD_ALL // CHILDREN)
    owners = jax.vmap(lambda own, number: assign_block(jax.random.fold_in(arg_keys[2], 2), own, number, CHILDREN, DEVICES, 1, CAP, 2))(owners_keys, owners_turns).reshape((CHILD_ALL, 1))
    slots = with_ends(jax.random.randint(arg_keys[3], (CHILD_ALL,), 1, BR * BC), jax.random.fold_in(arg_keys[3], 1), 1, (BR * BC) - 1).astype(jnp.int32)
    pattern = with_ends((jax.random.randint(arg_keys[4], (2, NB), 0, 2) < 1).astype(jnp.int32), jax.random.fold_in(arg_keys[4], 1), 0, 1)
    return dict(front=front, child_blocks=child_blocks, owners=owners, slots=slots, pattern=pattern)


def to_matrix(blocks):
    shape = blocks.shape
    moved = jnp.transpose(blocks, (0, 1, 4, 2, 3, 5))
    return moved.reshape(shape[0] * shape[1] * shape[4], shape[2] * shape[3] * shape[5])

def to_blocks(matrix):
    grouped = matrix.reshape(BR, PROWS, TILE, BC, PCOLS, TILE)
    return jnp.transpose(grouped, (0, 1, 3, 4, 2, 5))

def symmetric_lower(square):
    return jnp.tril(square) + jnp.tril(square, -1).T

def reference(front, child_blocks, owners, slots, pattern):
    owner_ids = owners[:, 0]
    row_owner = owner_ids // PCOLS
    col_owner = owner_ids % PCOLS
    local_row = slots // BC
    local_col = slots % BC
    flat_index = ((local_row * PROWS + row_owner) * BC + local_col) * PCOLS + col_owner
    assembled = front.reshape(-1, TILE, TILE).at[flat_index].add(child_blocks)
    matrix = to_matrix(assembled.reshape(front.shape))
    block_row = jnp.arange(NB * TILE, dtype=jnp.int32) // TILE
    patterns = (pattern[0], jnp.maximum(pattern[0], pattern[1]))
    factors = []
    for panel_idx in range(2):
        start = panel_idx * PANEL
        stop = start + PANEL
        column = matrix[:, start:stop]
        factor = jnp.linalg.cholesky(symmetric_lower(column[start:stop]))
        solved = jax.scipy.linalg.solve_triangular(factor, column.T, lower=True).T
        solved = solved.at[start:stop].set(factor)
        own_rows = (block_row >= 2 * panel_idx) & (block_row < 2 * panel_idx + 2)
        chosen = patterns[panel_idx][block_row].astype(jnp.float32)
        keep_rows = jnp.where(own_rows, 1.0, jnp.where(block_row < 2 * panel_idx, 0.0, chosen))
        lower_rows = solved * keep_rows[:, None]
        tail = lower_rows[stop:]
        matrix = matrix.at[stop:, stop:].add(-jnp.dot(tail, tail.T, precision=lax.Precision.HIGHEST))
        factors.append(lower_rows)
    lead = 2 * PANEL
    result = matrix.at[:, :lead].set(jnp.concatenate(factors, axis=1))
    result = result.at[:lead, lead:].set(0.0)
    return to_blocks(result)
```

```python
import functools

import jax
import jax.numpy as jnp
from jax import lax
from jax.experimental import pallas as pl
from jax.experimental.pallas import tpu as pltpu
from jax.sharding import PartitionSpec as P

ALL = ("prow", "pcol")
CHUNKS = 4
HIGHEST = lax.Precision.HIGHEST
VMEM_LIMIT = 56 * 2**20


def bits_of(size):
    return size.bit_length() - 1


def xor_send(x, axis, bit):
    size = lax.axis_size(axis)
    return lax.ppermute(x, axis, [(i, i ^ (1 << bit)) for i in range(size)])


def my_bit(axis, bit):
    return (lax.axis_index(axis) >> bit) & 1


def gather_bit(x, axis, bit):
    other = xor_send(x, axis, bit)
    low = my_bit(axis, bit) == 0
    return jnp.stack([jnp.where(low, x, other), jnp.where(low, other, x)])


def swap_bit(x, axis, bit):
    low = my_bit(axis, bit) == 0
    other = xor_send(jnp.where(low, x[1], x[0]), axis, bit)
    kept = jnp.where(low, x[0], x[1])
    return jnp.stack([jnp.where(low, kept, other), jnp.where(low, other, kept)])


def spread_high(x, axis, low_bits):
    for bit in range(low_bits, bits_of(lax.axis_size(axis))):
        other = lax.ppermute(x, axis, [(i, i | (1 << bit)) for i in range(1 << bit)])
        x = jnp.where(my_bit(axis, bit) == 1, other, x)
    return x


def nt_dot(a, b):
    return lax.dot_general(a, b, (((1,), (1,)), ((), ())), preferred_element_type=jnp.float32)


def split(x):
    high = x.astype(jnp.bfloat16)
    return high, (x - high.astype(jnp.float32)).astype(jnp.bfloat16)


def nt_dot3(a_high, a_low, b_high, b_low):
    return nt_dot(a_high, b_high) + (nt_dot(a_low, b_high) + nt_dot(a_high, b_low))


def pack_kernel(owner_ref, rank_ref, child_ref, first_ref, second_ref, sem):
    count = child_ref.shape[0]

    def to_first(k):
        return pltpu.make_async_copy(child_ref.at[k], first_ref.at[owner_ref[k]], sem.at[k])

    def to_second(k):
        return pltpu.make_async_copy(child_ref.at[k], second_ref.at[owner_ref[k]], sem.at[k])

    for k in range(count):
        pl.when(rank_ref[k] == 0)(lambda k=k: to_first(k).start())
        pl.when(rank_ref[k] != 0)(lambda k=k: to_second(k).start())
    for k in range(count):
        pl.when(rank_ref[k] == 0)(lambda k=k: to_first(k).wait())
        pl.when(rank_ref[k] != 0)(lambda k=k: to_second(k).wait())


def pack(owner_ids, rank, child_blocks, devices):
    count, tile, _ = child_blocks.shape
    shape = jax.ShapeDtypeStruct((devices, tile, tile), jnp.float32)
    return pl.pallas_call(
        pack_kernel,
        out_shape=(shape, shape),
        grid_spec=pltpu.PrefetchScalarGridSpec(
            num_scalar_prefetch=2,
            grid=(),
            in_specs=[pl.BlockSpec(memory_space=pl.ANY)],
            out_specs=(pl.BlockSpec(memory_space=pl.ANY), pl.BlockSpec(memory_space=pl.ANY)),
            scratch_shapes=[pltpu.SemaphoreType.DMA((count,))],
        ),
        name="pack_children",
    )(owner_ids, rank, child_blocks)


def strip_kernel(bcols, row_ref, strip_ref, got_ref, *rest):
    outs, (buffer, sem) = rest[:-2], rest[-2:]
    sources = got_ref.shape[0]
    brows = strip_ref.shape[0]
    depth = brows // len(outs)

    def copy(s):
        return pltpu.make_async_copy(got_ref.at[s], buffer.at[s], sem.at[s])

    for s in range(sources):
        pl.when(row_ref[s] >= 0)(lambda s=s: copy(s).start())
    for index, out in enumerate(outs):
        out[...] = strip_ref[index * depth : (index + 1) * depth]

    for s in range(sources):

        @pl.when(row_ref[s] >= 0)
        def _(s=s):
            copy(s).wait()
            for index, out in enumerate(outs):
                at = row_ref[s] - index * depth

                @pl.when((at >= 0) & (at < depth))
                def _():
                    place = jnp.clip(at, 0, depth - 1)
                    out[place] = out[place] + buffer[s]


def add_to_strip(panel_row, strip, got, bcols):
    brows, tile, _ = strip.shape
    shape = jax.ShapeDtypeStruct((brows // CHUNKS, tile, tile), jnp.float32)
    return pl.pallas_call(
        functools.partial(strip_kernel, bcols),
        out_shape=(shape,) * CHUNKS,
        grid_spec=pltpu.PrefetchScalarGridSpec(
            num_scalar_prefetch=1,
            grid=(),
            in_specs=[pl.BlockSpec(memory_space=pltpu.VMEM), pl.BlockSpec(memory_space=pl.ANY)],
            out_specs=(pl.BlockSpec(memory_space=pltpu.VMEM),) * CHUNKS,
            scratch_shapes=[
                pltpu.VMEM(got.shape, jnp.float32),
                pltpu.SemaphoreType.DMA((got.shape[0],)),
            ],
        ),
        compiler_params=pltpu.CompilerParams(vmem_limit_bytes=VMEM_LIMIT),
        name="add_panel_children",
    )(panel_row, strip, got)


def solve_rows(x, keep0, keep1, z0, a, z1):
    width = x.shape[1] // 2
    q0 = nt_dot3(*split(x[:, :width]), *z0) * keep0
    q0_parts = split(q0)
    rest = x[:, width:] - nt_dot3(*q0_parts, *a)
    q1 = nt_dot3(*split(rest), *z1) * keep1
    return q0, q1, q0_parts, split(q1)


def solve_kernel(with_panel, keep0_ref, keep1_ref, place_ref, x_ref, z_ref, high_ref, low_ref, *rest):
    n = pl.program_id(0)
    tile = x_ref.shape[-1]
    x = jnp.concatenate([x_ref[s % 2, s // 2, 0, 0] for s in range(4)], axis=1)
    factors = [(z_ref[2 * i], z_ref[2 * i + 1]) for i in range(3)]
    keep0 = keep0_ref[n].astype(jnp.float32)
    keep1 = keep1_ref[n].astype(jnp.float32)
    q0, q1, q0_parts, q1_parts = solve_rows(x, keep0, keep1, *factors)
    high_ref[...] = jnp.concatenate([q0_parts[0], q1_parts[0]], axis=1)
    low_ref[...] = jnp.concatenate([q0_parts[1], q1_parts[1]], axis=1)
    if with_panel:
        panel_ref, scratch = rest
        scratch[...] = jnp.concatenate([q0, q1], axis=1)
        panel_ref[0] = scratch[:, pl.ds(pl.multiple_of(place_ref[0] * tile, tile), tile)]


def solve(blocks, keep0, keep1, place, factors, with_panel):
    _, _, high, rows, tile, _ = blocks.shape
    count = high * rows
    width = 4 * tile
    part = jax.ShapeDtypeStruct((count * tile, width), jnp.bfloat16)
    row_spec = pl.BlockSpec((tile, width), lambda n, *_: (n, 0))
    out_shape, out_specs, scratch = [part, part], [row_spec, row_spec], []
    if with_panel:
        out_shape.append(jax.ShapeDtypeStruct((count, tile, tile), jnp.float32))
        out_specs.append(pl.BlockSpec((1, tile, tile), lambda n, *_: (n, 0, 0)))
        scratch.append(pltpu.VMEM((tile, width), jnp.float32))
    return pl.pallas_call(
        functools.partial(solve_kernel, with_panel),
        out_shape=tuple(out_shape),
        grid_spec=pltpu.PrefetchScalarGridSpec(
            num_scalar_prefetch=3,
            grid=(count,),
            in_specs=[
                pl.BlockSpec((2, 2, 1, 1, tile, tile), lambda n, *_: (0, 0, n % high, n // high, 0, 0)),
                pl.BlockSpec(factors.shape, lambda n, *_: (0, 0, 0)),
            ],
            out_specs=tuple(out_specs),
            scratch_shapes=scratch,
        ),
        compiler_params=pltpu.CompilerParams(vmem_limit_bytes=VMEM_LIMIT),
        name="solve_rows" if with_panel else "solve_columns",
    )(keep0, keep1, place, blocks, factors)


def final_kernel(bcols, panel_blocks, first_ref, second_ref, place_ref, front_ref, got1_ref, got2_ref, high_ref, low_ref,
                 panel_ref, corner_ref, *rest):
    cols, out_ref = rest[:-1], rest[-1]
    step = pl.program_id(0)
    depth = front_ref.shape[0]
    tile = front_ref.shape[-1]
    my_row, my_col, grid_rows = place_ref[0], place_ref[1], place_ref[2]
    at = 0
    for index in range(len(cols) // 2):
        col_high, col_low = cols[2 * index], cols[2 * index + 1]
        blocks = col_high.shape[0] // tile
        update = nt_dot3(high_ref[...], low_ref[...], col_high[...], col_low[...])
        for a in range(depth):
            for b in range(blocks):
                out_ref[a, 0, at + b, 0] = (
                    front_ref[a, 0, at + b, 0] - update[a * tile : (a + 1) * tile, b * tile : (b + 1) * tile]
                )
        at += blocks

    def add(slot_ref, got_ref):
        def body(s, carry):
            slot = slot_ref[s]
            a = slot // bcols - step * depth

            @pl.when((slot > 0) & (a >= 0) & (a < depth))
            def _():
                out_ref[a, 0, slot % bcols, 0] = out_ref[a, 0, slot % bcols, 0] + got_ref[s]

            return carry

        lax.fori_loop(0, got_ref.shape[0], body, 0)

    add(first_ref, got1_ref)
    add(second_ref, got2_ref)

    for a in range(depth):
        block_row = (step * depth + a) * grid_rows + my_row

        @pl.when(block_row < panel_blocks)
        def _(a=a):
            out_ref[a] = jnp.zeros(out_ref.shape[1:], jnp.float32)

        @pl.when(my_col < panel_blocks)
        def _(a=a):
            out_ref[a, 0, 0, 0] = jnp.where(block_row < panel_blocks, corner_ref[...], panel_ref[a])


def finish(first, second, place, front, got1, got2, row_high, row_low, panel, corner, cols, panel_blocks):
    brows, _, bcols, _, tile, _ = front.shape
    depth = 2
    whole = pl.BlockSpec(memory_space=pltpu.VMEM)
    big = pl.BlockSpec((depth, 1, bcols, 1, tile, tile), lambda i, *_: (i, 0, 0, 0, 0, 0))
    rows = pl.BlockSpec((depth * tile, row_high.shape[1]), lambda i, *_: (i, 0))
    return pl.pallas_call(
        functools.partial(final_kernel, bcols, panel_blocks),
        out_shape=jax.ShapeDtypeStruct(front.shape, jnp.float32),
        grid_spec=pltpu.PrefetchScalarGridSpec(
            num_scalar_prefetch=3,
            grid=(brows // depth,),
            in_specs=[big, whole, whole, rows, rows, pl.BlockSpec((depth, tile, tile), lambda i, *_: (i, 0, 0)), whole]
            + [whole] * len(cols),
            out_specs=big,
        ),
        compiler_params=pltpu.CompilerParams(vmem_limit_bytes=VMEM_LIMIT),
        name="schur_update",
    )(first, second, place, front, got1, got2, row_high, row_low, panel, corner, *cols)


def symmetric_lower(square):
    return jnp.tril(square) + jnp.tril(square, -1).T


def factor(leading, pattern, tile):
    width = leading.shape[0] // 2
    identity = jnp.eye(width, dtype=jnp.float32)

    def step(square):
        lower = jnp.linalg.cholesky(symmetric_lower(square))
        return lower, jax.scipy.linalg.solve_triangular(lower, identity, lower=True)

    l0, z0 = step(leading[:width, :width])
    keep = jnp.repeat(pattern[0, 2:4].astype(jnp.float32), tile)
    a = jnp.dot(leading[width:, :width], z0.T, precision=HIGHEST) * keep[:, None]
    l1, z1 = step(leading[width:, width:] - jnp.dot(a, a.T, precision=HIGHEST))
    return l0, a, l1, z0, z1


def local(front, child_blocks, owners, slots, pattern):
    grid_rows = lax.axis_size("prow")
    grid_cols = lax.axis_size("pcol")
    devices = grid_rows * grid_cols
    rank_r = lax.axis_index("prow")
    rank_c = lax.axis_index("pcol")
    me = rank_r * grid_cols + rank_c
    brows, _, bcols, _, tile, _ = front.shape
    row_bits, col_bits = bits_of(grid_rows), bits_of(grid_cols)
    panel_blocks = 2 * pattern.shape[0]
    panel_bits = bits_of(panel_blocks)
    owner_ids = owners[:, 0]
    children = owner_ids.shape[0]

    def ranks(owner, slot):
        panel = (slot % bcols == 0) & (owner % grid_cols < panel_blocks)
        same = owner[..., :, None] == owner[..., None, :]
        index = jnp.arange(children, dtype=jnp.int32)
        ahead = jnp.where(
            panel[..., :, None] == panel[..., None, :], index[None, :] < index[:, None], panel[..., None, :]
        )
        return jnp.sum((same & ahead).astype(jnp.int32), axis=-1), panel

    rank, _ = ranks(owner_ids, slots)
    send1, send2 = pack(owner_ids, rank, child_blocks, devices)
    got1 = lax.all_to_all(send1, ALL, 0, 0, tiled=True)

    corner = front[0, 0, 0, 0]
    corner = spread_high(corner, "prow", panel_bits)
    corner = spread_high(corner, "pcol", panel_bits)
    for bit in reversed(range(panel_bits)):
        corner = gather_bit(corner, "prow", bit)
    for bit in reversed(range(panel_bits)):
        corner = gather_bit(corner, "pcol", bit)
    leading = jnp.transpose(corner, (3, 2, 4, 1, 0, 5)).reshape(panel_blocks * tile, panel_blocks * tile)
    l0, a, l1, z0, z1 = factor(leading, pattern, tile)
    highs = [lax.reduce_precision(whole, 8, 7) for whole in (z0, a, z1)]
    lows = [whole - high for whole, high in zip((z0, a, z1), highs)]
    factors = jnp.stack([part for pair in zip(highs, lows) for part in pair]).astype(jnp.bfloat16)
    corners = jnp.concatenate(
        [jnp.concatenate([l0, jnp.zeros_like(l0)], axis=1), jnp.concatenate([a, l1], axis=1)], axis=0
    ).reshape(panel_blocks, tile, panel_blocks, tile)
    own_row = jnp.minimum(rank_r, panel_blocks - 1)
    own_col = jnp.minimum(rank_c, panel_blocks - 1)
    own_corner = corners[own_row, :, own_col, :]

    every = lax.all_gather(jnp.stack([owner_ids, slots]), ALL)
    every_owner, every_slot = every[:, 0], every[:, 1]
    every_rank, every_panel = ranks(every_owner, every_slot)
    mine = every_owner == me
    trail_slot = jnp.where(mine & ~every_panel, every_slot, 0)
    first_slots = jnp.sum(jnp.where(every_rank == 0, trail_slot, 0), axis=1)
    second_slots = jnp.sum(jnp.where(every_rank == 1, trail_slot, 0), axis=1)
    panel_row = jnp.sum(jnp.where(mine & every_panel & (every_rank == 0), every_slot // bcols + 1, 0), axis=1) - 1

    strip = front[:, 0, 0, 0]
    late = every_panel & (every_rank == 1)
    order = jnp.cumsum(late.astype(jnp.int32), axis=1)
    rounds = jnp.max(order[:, -1])

    def deliver(turn, strip):
        chosen = late & (order == turn + 1)
        block = child_blocks[jnp.argmax(chosen[me])]
        for axis, bits in (("prow", row_bits), ("pcol", col_bits)):
            for bit in reversed(range(bits)):
                block = gather_bit(block, axis, bit)
        bits = row_bits + col_bits
        blocks = jnp.transpose(block, tuple(reversed(range(bits))) + (bits, bits + 1)).reshape(devices, tile, tile)
        here = jnp.any(chosen & mine, axis=1)
        rows = jnp.sum(jnp.where(chosen & mine, every_slot // bcols, 0), axis=1)
        return strip.at[rows].add(jnp.where(here[:, None, None], blocks, 0.0))

    strip = lax.fori_loop(0, rounds, deliver, strip)

    chunks = add_to_strip(panel_row, strip, got1, bcols)
    got2 = lax.all_to_all(send2, ALL, 0, 0, tiled=True)
    keep = (pattern[0], jnp.maximum(pattern[0], pattern[1]))
    place = jnp.stack([rank_r, rank_c, jnp.int32(grid_rows)])
    high_count = grid_rows // grid_cols
    high_bits = row_bits - col_bits
    depth = brows // CHUNKS
    cols, row_parts = [], []
    for index, chunk in enumerate(chunks):
        rows = jnp.arange(index * depth, (index + 1) * depth, dtype=jnp.int32)
        chunk = spread_high(chunk, "pcol", panel_bits)
        row = chunk
        for bit in reversed(range(panel_bits)):
            row = gather_bit(row, "pcol", bit)
        row_parts.append(row)
        x = chunk
        for bit in reversed(range(row_bits)):
            x = gather_bit(x, "prow", bit)
            if bit < panel_bits:
                x = swap_bit(x, "pcol", bit)
            elif bit < col_bits:
                x = jnp.where(my_bit("pcol", bit) == 0, x[0], x[1])
        x = jnp.transpose(
            x, (0, 1) + tuple(reversed(range(2, 2 + high_bits))) + tuple(range(2 + high_bits, 5 + high_bits))
        ).reshape(2, 2, high_count, depth, tile, tile)
        blocks = (rows[:, None] * grid_rows + jnp.arange(high_count, dtype=jnp.int32) * grid_cols + rank_c).reshape(-1)
        cols += solve(x, keep[0][blocks], keep[1][blocks], rank_c[None], factors, False)
    row = jnp.concatenate(row_parts, axis=2)[:, :, None]
    blocks = jnp.arange(brows, dtype=jnp.int32) * grid_rows + rank_r
    row_high, row_low, panel = solve(row, keep[0][blocks], keep[1][blocks], own_col[None], factors, True)
    return finish(
        first_slots, second_slots, place, front, got1, got2, row_high, row_low, panel, own_corner, cols, panel_blocks
    )


def solution(mesh):
    placed = (
        P(None, "prow", None, "pcol", None, None),
        P(("prow", "pcol"), None, None),
        P(("prow", "pcol"), None),
        P(("prow", "pcol")),
        P(),
    )
    return jax.shard_map(
        local,
        mesh=mesh,
        in_specs=placed,
        out_specs=P(None, "prow", None, "pcol", None, None),
        check_vma=False,
    )
```

```python
import functools

import jax
import jax.numpy as jnp
from jax import lax
from jax.experimental import pallas as pl
from jax.experimental.pallas import tpu as pltpu
from jax.sharding import PartitionSpec as P

ALL = ("prow", "pcol")
HIGHEST = lax.Precision.HIGHEST
VMEM_LIMIT = 56 * 2**20
WHOLE = pl.BlockSpec(memory_space=pltpu.VMEM)
HBM = pl.BlockSpec(memory_space=pl.ANY)


def bits_of(size):
    return size.bit_length() - 1


def xor_send(x, axis, bit):
    size = lax.axis_size(axis)
    return lax.ppermute(x, axis, [(i, i ^ (1 << bit)) for i in range(size)])


def my_bit(axis, bit):
    return (lax.axis_index(axis) >> bit) & 1


def gather_bit(x, axis, bit):
    other = xor_send(x, axis, bit)
    low = my_bit(axis, bit) == 0
    return jnp.stack([jnp.where(low, x, other), jnp.where(low, other, x)])


def spread_high(x, axis, low_bits):
    for bit in range(low_bits, bits_of(lax.axis_size(axis))):
        other = lax.ppermute(x, axis, [(i, i | (1 << bit)) for i in range(1 << bit)])
        x = jnp.where(my_bit(axis, bit) == 1, other, x)
    return x


def nt_dot(a, b):
    return lax.dot_general(a, b, (((1,), (1,)), ((), ())), preferred_element_type=jnp.float32)


def split(x):
    high = x.astype(jnp.bfloat16)
    return high, (x - high.astype(jnp.float32)).astype(jnp.bfloat16)


def nt_dot3(a, b):
    return nt_dot(a[0], b[0]) + (nt_dot(a[1], b[0]) + nt_dot(a[0], b[1]))


def pack_kernel(owner_ref, rank_ref, child_ref, first_ref, second_ref, sem):
    count = child_ref.shape[0]

    def to_first(k):
        return pltpu.make_async_copy(child_ref.at[k], first_ref.at[owner_ref[k]], sem.at[k])

    def to_second(k):
        return pltpu.make_async_copy(child_ref.at[k], second_ref.at[owner_ref[k]], sem.at[k])

    for k in range(count):
        pl.when(rank_ref[k] == 0)(lambda k=k: to_first(k).start())
        pl.when(rank_ref[k] != 0)(lambda k=k: to_second(k).start())
    for k in range(count):
        pl.when(rank_ref[k] == 0)(lambda k=k: to_first(k).wait())
        pl.when(rank_ref[k] != 0)(lambda k=k: to_second(k).wait())


def pack(owner_ids, rank, child_blocks, devices):
    count, tile, _ = child_blocks.shape
    shape = jax.ShapeDtypeStruct((devices, tile, tile), jnp.float32)
    return pl.pallas_call(
        pack_kernel,
        out_shape=(shape, shape),
        grid_spec=pltpu.PrefetchScalarGridSpec(
            num_scalar_prefetch=2,
            grid=(),
            in_specs=[WHOLE],
            out_specs=(HBM, HBM),
            scratch_shapes=[pltpu.SemaphoreType.DMA((count,))],
        ),
        compiler_params=pltpu.CompilerParams(vmem_limit_bytes=VMEM_LIMIT),
        name="pack_children",
    )(owner_ids, rank, child_blocks)


def strip_kernel(row_ref, strip_ref, got_ref, out_ref, buffer, sem):
    sources = got_ref.shape[0]

    def copy(s):
        return pltpu.make_async_copy(got_ref.at[s], buffer.at[s], sem.at[s])

    for s in range(sources):
        pl.when(row_ref[s] >= 0)(lambda s=s: copy(s).start())
    out_ref[...] = strip_ref[...]
    for s in range(sources):

        @pl.when(row_ref[s] >= 0)
        def _(s=s):
            copy(s).wait()
            out_ref[row_ref[s]] = out_ref[row_ref[s]] + buffer[s]


def add_to_strip(panel_row, strip, got):
    return pl.pallas_call(
        strip_kernel,
        out_shape=jax.ShapeDtypeStruct(strip.shape, jnp.float32),
        grid_spec=pltpu.PrefetchScalarGridSpec(
            num_scalar_prefetch=1,
            grid=(),
            in_specs=[WHOLE, HBM],
            out_specs=WHOLE,
            scratch_shapes=[
                pltpu.VMEM(got.shape, jnp.float32),
                pltpu.SemaphoreType.DMA((got.shape[0],)),
            ],
        ),
        compiler_params=pltpu.CompilerParams(vmem_limit_bytes=VMEM_LIMIT),
        name="add_panel_children",
    )(panel_row, strip, got)


def exact_dot(a, b, dims):
    return lax.dot_general(a, b, (dims, ((), ())), precision=HIGHEST, preferred_element_type=jnp.float32)


def inverse_root(x):
    y = lax.rsqrt(x)
    return y * (1.5 - 0.5 * x * y * y)


def eliminate(work_ref, right_ref, t_ref, z_ref):
    n = work_ref.shape[0]
    row = lax.broadcasted_iota(jnp.int32, (n, n), 0)
    col = lax.broadcasted_iota(jnp.int32, (n, n), 1)
    right_ref[...] = jnp.where(row == col, 1.0, 0.0)
    for j in range(0, n, 2):
        lo = j // 8 * 8
        i = j - lo
        a = work_ref[lo:, :]
        z = right_ref[lo:, :]
        col0 = jnp.broadcast_to(a[:, j : j + 1], a.shape)
        col1 = jnp.broadcast_to(a[:, j + 1 : j + 2], a.shape)
        inv0 = inverse_root(col0[i : i + 1, :])
        row0 = a[i : i + 1, :] * inv0
        low0 = col0 * inv0
        cross = low0[i + 1 : i + 2, :]
        low1 = col1 - low0 * cross
        inv1 = inverse_root(low1[i + 1 : i + 2, :])
        row1 = (a[i + 1 : i + 2, :] - cross * row0) * inv1
        low1 = low1 * inv1
        z0 = z[i : i + 1, :] * inv0
        z1 = (z[i + 1 : i + 2, :] - cross * z0) * inv1
        if j + 2 < n:
            work_ref[lo:, :] = a - low0 * row0 - low1 * row1
            right_ref[lo:, :] = z - low0 * z0 - low1 * z1
        t_ref[j : j + 1, :] = row0
        t_ref[j + 1 : j + 2, :] = row1
        z_ref[j : j + 1, :] = z0
        z_ref[j + 1 : j + 2, :] = z1


def lower_of(t):
    n = t.shape[0]
    row = lax.broadcasted_iota(jnp.int32, (n, n), 0)
    col = lax.broadcasted_iota(jnp.int32, (n, n), 1)
    return jnp.where(col <= row, t.T, 0.0)


def symmetric(block):
    n = block.shape[0]
    row = lax.broadcasted_iota(jnp.int32, (n, n), 0)
    col = lax.broadcasted_iota(jnp.int32, (n, n), 1)
    return jnp.where(col <= row, block, block.T)


def factor_panel(g, scratch):
    work, right, t, z = scratch
    nt, nn = ((1,), (1,)), ((1,), (0,))
    work[...] = symmetric(g[0][0])
    eliminate(work, right, t, z)
    l00, z00 = lower_of(t[...]), z[...]
    l10 = exact_dot(g[1][0], z00, nt)
    work[...] = symmetric(g[1][1]) - exact_dot(l10, l10, nt)
    eliminate(work, right, t, z)
    l11, z11 = lower_of(t[...]), z[...]
    z10 = -exact_dot(z11, exact_dot(l10, z00, nn), nn)
    return (l00, l10, l11), (z00, z10, z11)


def store_square(ref, blocks):
    tile = blocks[0].shape[0]
    ref[:tile, :tile] = blocks[0]
    ref[:tile, tile:] = jnp.zeros((tile, tile), ref.dtype)
    ref[tile:, :tile] = blocks[1]
    ref[tile:, tile:] = blocks[2]


def leading_block(ref, i, j):
    return ref[j % 2, j // 2, i % 2, i // 2]


def panel0_kernel(corner_ref, l_ref, zh_ref, zl_ref, *scratch):
    g = [[leading_block(corner_ref, i, j) for j in range(2)] for i in range(2)]
    lower, inverse = factor_panel(g, scratch)
    store_square(l_ref, lower)
    parts = [split(block) for block in inverse]
    store_square(zh_ref, [part[0] for part in parts])
    store_square(zl_ref, [part[1] for part in parts])


def panel1_kernel(keep_ref, corner_ref, z0h_ref, z0l_ref, a_ref, ah_ref, al_ref, l_ref, zh_ref, zl_ref, *scratch):
    tile = corner_ref.shape[-1]
    z0 = (z0h_ref[...], z0l_ref[...])
    rows = [jnp.concatenate([leading_block(corner_ref, 2 + i, j) for j in range(2)], axis=1) for i in range(2)]
    a = jnp.concatenate([nt_dot3(split(rows[i]), z0) * keep_ref[i].astype(jnp.float32) for i in range(2)], axis=0)
    a_ref[...] = a
    ah_ref[...], al_ref[...] = split(a)
    update = exact_dot(a, a, ((1,), (1,)))
    g = [
        [leading_block(corner_ref, 2 + i, 2 + j) - update[i * tile : (i + 1) * tile, j * tile : (j + 1) * tile] for j in range(2)]
        for i in range(2)
    ]
    lower, inverse = factor_panel(g, scratch)
    store_square(l_ref, lower)
    parts = [split(block) for block in inverse]
    store_square(zh_ref, [part[0] for part in parts])
    store_square(zl_ref, [part[1] for part in parts])


def factor_leading(corner, keep):
    tile = corner.shape[-1]
    width = 2 * tile
    full = jax.ShapeDtypeStruct((width, width), jnp.float32)
    part = jax.ShapeDtypeStruct((width, width), jnp.bfloat16)
    scratch = [pltpu.VMEM((tile, tile), jnp.float32)] * 4
    l0, z0h, z0l = pl.pallas_call(
        panel0_kernel,
        out_shape=(full, part, part),
        in_specs=[WHOLE],
        out_specs=(WHOLE,) * 3,
        scratch_shapes=scratch,
        compiler_params=pltpu.CompilerParams(vmem_limit_bytes=VMEM_LIMIT),
        name="factor_panel0",
    )(corner)
    a, ah, al, l1, z1h, z1l = pl.pallas_call(
        panel1_kernel,
        out_shape=(full, part, part, full, part, part),
        grid_spec=pltpu.PrefetchScalarGridSpec(
            num_scalar_prefetch=1, grid=(), in_specs=[WHOLE] * 3, out_specs=(WHOLE,) * 6, scratch_shapes=scratch
        ),
        compiler_params=pltpu.CompilerParams(vmem_limit_bytes=VMEM_LIMIT),
        name="factor_panel1",
    )(keep, corner, z0h, z0l)
    return l0, a, l1, (z0h, z0l, ah, al, z1h, z1l)


def solve_kernel(with_panel, keep0_ref, keep1_ref, place_ref, *refs):
    x_refs, factor_refs, rest = refs[:4], refs[4:10], refs[10:]
    high_ref, low_ref, xs = rest[0], rest[1], rest[-1]
    n = pl.program_id(0)
    depth, tile, _ = x_refs[0].shape
    for m in range(4):
        xs[place_ref[0] ^ m] = x_refs[m][...].reshape(depth * tile, tile)
    z0, a, z1 = [(factor_refs[2 * i][...], factor_refs[2 * i + 1][...]) for i in range(3)]

    def masked(q, keep_ref):
        return jnp.concatenate(
            [q[i * tile : (i + 1) * tile] * keep_ref[n * depth + i].astype(jnp.float32) for i in range(depth)], axis=0
        )

    x0 = jnp.concatenate([xs[0], xs[1]], axis=1)
    x1 = jnp.concatenate([xs[2], xs[3]], axis=1)
    q0 = masked(nt_dot3(split(x0), z0), keep0_ref)
    q0_parts = split(q0)
    q1 = masked(nt_dot3(split(x1 - nt_dot3(q0_parts, a)), z1), keep1_ref)
    q1_parts = split(q1)
    width = 2 * tile
    for ref, index in ((high_ref, 0), (low_ref, 1)):
        ref[:, :width] = q0_parts[index]
        ref[:, width:] = q1_parts[index]
    if with_panel:
        xs[0] = q0[:, :tile]
        xs[1] = q0[:, tile:]
        xs[2] = q1[:, :tile]
        xs[3] = q1[:, tile:]
        rest[2][...] = xs[place_ref[0]].reshape(depth, tile, tile)


def solve(strips, keep0, keep1, place, factors, with_panel):
    rows, tile, _ = strips[0].shape
    depth = rows // 2
    part = jax.ShapeDtypeStruct((rows * tile, 4 * tile), jnp.bfloat16)
    row_spec = pl.BlockSpec((depth * tile, 4 * tile), lambda n, *_: (n, 0))
    strip_spec = pl.BlockSpec((depth, tile, tile), lambda n, *_: (n, 0, 0))
    out_shape, out_specs = [part, part], [row_spec, row_spec]
    if with_panel:
        out_shape.append(jax.ShapeDtypeStruct((rows, tile, tile), jnp.float32))
        out_specs.append(strip_spec)
    return pl.pallas_call(
        functools.partial(solve_kernel, with_panel),
        out_shape=tuple(out_shape),
        grid_spec=pltpu.PrefetchScalarGridSpec(
            num_scalar_prefetch=3,
            grid=(rows // depth,),
            in_specs=[strip_spec] * 4 + [WHOLE] * 6,
            out_specs=tuple(out_specs),
            scratch_shapes=[pltpu.VMEM((4, depth * tile, tile), jnp.float32)],
        ),
        compiler_params=pltpu.CompilerParams(vmem_limit_bytes=VMEM_LIMIT),
        name="solve_rows" if with_panel else "solve_columns",
    )(keep0, keep1, place, *strips, *factors)


def final_kernel(panel_blocks, first_ref, second_ref, place_ref, front_ref, got1_ref, got2_ref, high_ref, low_ref,
                 panel_ref, l0_ref, a_ref, l1_ref, *rest):
    cols, out_ref = rest[:-1], rest[-1]
    step = pl.program_id(0)
    depth, _, bcols, _, tile, _ = front_ref.shape
    my_row, my_col, grid_rows, my_high = place_ref[0], place_ref[1], place_ref[2], place_ref[3]
    highs = len(cols) // 2
    rows = (high_ref[...], low_ref[...])
    for index in range(highs):
        col_high, col_low = cols[2 * index], cols[2 * index + 1]
        for at in range(0, bcols // highs, 2):
            piece = slice(at * tile, (at + 2) * tile)
            update = nt_dot3(rows, (col_high[piece, :], col_low[piece, :]))
            for k in range(2):
                b = (at + k) * highs + (my_high ^ index)
                for a in range(depth):
                    out_ref[a, 0, b, 0] = (
                        front_ref[a, 0, b, 0] - update[a * tile : (a + 1) * tile, k * tile : (k + 1) * tile]
                    )

    def add(list_ref, got_ref):
        def body(k, carry):
            slot = list_ref[1, k]
            a, b = slot // bcols - step * depth, slot % bcols
            out_ref[a, 0, b, 0] = out_ref[a, 0, b, 0] + got_ref[list_ref[0, k]]
            return carry

        lax.fori_loop(list_ref[2, step], list_ref[2, step + 1], body, 0)

    add(first_ref, got1_ref)
    add(second_ref, got2_ref)

    for a in range(depth):
        block_row = (step * depth + a) * grid_rows + my_row

        @pl.when(block_row < panel_blocks)
        def _(a=a):
            out_ref[a] = jnp.zeros(out_ref.shape[1:], jnp.float32)

        @pl.when(my_col < panel_blocks)
        def _(a=a):
            out_ref[a, 0, 0, 0] = panel_ref[a]

        for i in range(panel_blocks):
            for j in range(panel_blocks):

                @pl.when((block_row == i) & (my_col == j))
                def _(a=a, i=i, j=j):
                    ref = (l0_ref, None, a_ref, l1_ref)[i // 2 * 2 + j // 2]
                    rows_at, cols_at = i % 2 * tile, j % 2 * tile
                    if ref is None:
                        out_ref[a, 0, 0, 0] = jnp.zeros((tile, tile), jnp.float32)
                    else:
                        out_ref[a, 0, 0, 0] = ref[rows_at : rows_at + tile, cols_at : cols_at + tile]


def finish(depth, first, second, place, front, got1, got2, row_high, row_low, panel, corners, cols, panel_blocks):
    brows, _, bcols, _, tile, _ = front.shape
    big = pl.BlockSpec((depth, 1, bcols, 1, tile, tile), lambda i, *_: (i, 0, 0, 0, 0, 0))
    rows = pl.BlockSpec((depth * tile, row_high.shape[1]), lambda i, *_: (i, 0))
    return pl.pallas_call(
        functools.partial(final_kernel, panel_blocks),
        out_shape=jax.ShapeDtypeStruct(front.shape, jnp.float32),
        grid_spec=pltpu.PrefetchScalarGridSpec(
            num_scalar_prefetch=3,
            grid=(brows // depth,),
            in_specs=[big, WHOLE, WHOLE, rows, rows, pl.BlockSpec((depth, tile, tile), lambda i, *_: (i, 0, 0))]
            + [WHOLE] * (3 + len(cols)),
            out_specs=big,
        ),
        compiler_params=pltpu.CompilerParams(vmem_limit_bytes=VMEM_LIMIT),
        name="schur_update",
    )(first, second, place, front, got1, got2, row_high, row_low, panel, *corners, *cols)


def by_slot(slots, per_step, steps):
    count = slots.shape[0]
    index = jnp.arange(count, dtype=jnp.int32)
    key = jnp.where(slots > 0, slots, per_step * steps) * count + index
    place = jnp.sum((key[None, :] < key[:, None]).astype(jnp.int32), axis=1)
    at = place[None, :] == index[:, None]
    sources = jnp.sum(jnp.where(at, index[None, :], 0), axis=1)
    ordered = jnp.sum(jnp.where(at, slots[None, :], 0), axis=1)
    bound = jnp.minimum(index, steps) * per_step
    starts = jnp.sum(((slots > 0)[None, :] & (slots[None, :] < bound[:, None])).astype(jnp.int32), axis=1)
    return jnp.stack([sources, ordered, starts])


def local(front, child_blocks, owners, slots, pattern):
    grid_rows = lax.axis_size("prow")
    grid_cols = lax.axis_size("pcol")
    devices = grid_rows * grid_cols
    rank_r = lax.axis_index("prow")
    rank_c = lax.axis_index("pcol")
    me = rank_r * grid_cols + rank_c
    brows, _, bcols, _, tile, _ = front.shape
    row_bits, col_bits = bits_of(grid_rows), bits_of(grid_cols)
    panel_blocks = 2 * pattern.shape[0]
    panel_bits = bits_of(panel_blocks)
    owner_ids = owners[:, 0]
    children = owner_ids.shape[0]

    index = jnp.arange(children, dtype=jnp.int32)
    is_panel = (slots % bcols == 0) & (owner_ids % grid_cols < panel_blocks)
    same = owner_ids[:, None] == owner_ids[None, :]
    ahead = jnp.where(is_panel[:, None] == is_panel[None, :], index[None, :] < index[:, None], is_panel[None, :])
    rank = jnp.sum((same & ahead).astype(jnp.int32), axis=1)
    late = is_panel & (rank == 1)

    to = owner_ids[None, :] == jnp.arange(devices, dtype=jnp.int32)[:, None]
    lane = jnp.arange(tile, dtype=jnp.int32)[None, :]
    slot1 = jnp.sum(jnp.where(to & (rank == 0)[None, :], slots[None, :], 0), axis=1, keepdims=True)
    slot2 = jnp.sum(jnp.where(to & (rank == 1)[None, :], slots[None, :], 0), axis=1, keepdims=True)
    late_count = jnp.sum(late.astype(jnp.int32))
    notes = jnp.where(lane == 0, slot1, jnp.where(lane == 1, slot2, late_count))
    got_notes = lax.all_to_all(notes[:, None, :], ALL, 0, 0, tiled=True)[:, 0]

    send1, send2 = pack(owner_ids, rank, child_blocks, devices)
    got1 = lax.all_to_all(send1, ALL, 0, 0, tiled=True)

    corner = front[0, 0, 0, 0]
    corner = spread_high(corner, "prow", panel_bits)
    corner = spread_high(corner, "pcol", panel_bits)
    for bit in reversed(range(panel_bits)):
        corner = gather_bit(corner, "prow", bit)
    for bit in reversed(range(panel_bits)):
        corner = gather_bit(corner, "pcol", bit)
    l0, a, l1, factors = factor_leading(corner, pattern[0, 2:4])

    first_slots, second_slots = got_notes[:, 0], got_notes[:, 1]

    def panel_here(slot):
        return (slot % bcols == 0) & (slot > 0) & (rank_c < panel_blocks)

    panel_row = jnp.where(panel_here(first_slots), first_slots // bcols, -1)
    depth = brows // 4
    lists = [by_slot(jnp.where(panel_here(s), 0, s), depth * bcols, brows // depth) for s in (first_slots, second_slots)]

    strip = front[:, 0, 0, 0]
    rounds = jnp.max(got_notes[:, 2])
    order = jnp.cumsum(late.astype(jnp.int32))

    def deliver(turn, strip):
        chosen = late & (order == turn + 1)
        block = child_blocks[jnp.argmax(chosen)]
        note = jnp.where(lane == 0, jnp.sum(jnp.where(chosen, owner_ids + 1, 0)), jnp.sum(jnp.where(chosen, slots, 0)))
        for axis, bits in (("prow", row_bits), ("pcol", col_bits)):
            for bit in reversed(range(bits)):
                block = gather_bit(block, axis, bit)
                note = gather_bit(note, axis, bit)
        bits = row_bits + col_bits
        blocks = block.reshape(devices, tile, tile)
        note = note.reshape(devices, tile)
        here = note[:, 0] == me + 1
        rows = jnp.where(here, note[:, 1] // bcols, 0)
        return strip.at[rows].add(jnp.where(here[:, None, None], blocks, 0.0))

    strip = lax.fori_loop(0, rounds, deliver, strip)
    strip = add_to_strip(panel_row, strip, got1)
    strip = spread_high(strip, "pcol", panel_bits)

    across = xor_send(strip, "pcol", 1)
    row_strips = [strip, xor_send(strip, "pcol", 0), across, xor_send(across, "pcol", 0)]
    parts = [strip]
    for bit in range(col_bits, row_bits):
        parts = parts + [xor_send(part, "prow", bit) for part in parts]
    highs = len(parts)

    def to_columns(part, m):
        pairs = [
            ((h * grid_cols + low) * grid_cols + c, (h * grid_cols + (c ^ m)) * grid_cols + low)
            for h in range(highs)
            for low in range(grid_cols)
            for c in range(grid_cols)
        ]
        return lax.ppermute(part, ALL, pairs)

    col_strips = [[to_columns(part, m) for m in range(panel_blocks)] for part in parts]
    got2 = lax.all_to_all(send2, ALL, 0, 0, tiled=True)

    keep0, keep1 = pattern[0], jnp.maximum(pattern[0], pattern[1])
    my_high = rank_r // grid_cols
    rows_of = jnp.arange(brows, dtype=jnp.int32) * grid_rows
    blocks = rows_of + rank_r
    row_high, row_low, panel = solve(
        row_strips, keep0[blocks], keep1[blocks], (rank_c % panel_blocks)[None], factors, True
    )
    cols = []
    for high, strips in enumerate(col_strips):
        blocks = rows_of + (my_high ^ high) * grid_cols + rank_c
        cols += solve(strips, keep0[blocks], keep1[blocks], (rank_r % panel_blocks)[None], factors, False)
    place = jnp.stack([rank_r, rank_c, jnp.int32(grid_rows), my_high])
    return finish(
        depth, *lists, place, front, got1, got2, row_high, row_low, panel, (l0, a, l1), cols, panel_blocks
    )


def solution(mesh):
    placed = (
        P(None, "prow", None, "pcol", None, None),
        P(("prow", "pcol"), None, None),
        P(("prow", "pcol"), None),
        P(("prow", "pcol")),
        P(),
    )
    return jax.shard_map(
        local,
        mesh=mesh,
        in_specs=placed,
        out_specs=P(None, "prow", None, "pcol", None, None),
        check_vma=False,
    )
```

```python
import functools

import jax
import jax.numpy as jnp
from jax import lax
from jax.experimental import pallas as pl
from jax.experimental.pallas import tpu as pltpu
from jax.sharding import PartitionSpec as P

ALL = ("prow", "pcol")
HIGHEST = lax.Precision.HIGHEST
VMEM_LIMIT = 56 * 2**20
WHOLE = pl.BlockSpec(memory_space=pltpu.VMEM)
HBM = pl.BlockSpec(memory_space=pl.ANY)


def bits_of(size):
    return size.bit_length() - 1


def xor_send(x, axis, bit):
    size = lax.axis_size(axis)
    return lax.ppermute(x, axis, [(i, i ^ (1 << bit)) for i in range(size)])


def my_bit(axis, bit):
    return (lax.axis_index(axis) >> bit) & 1


def gather_bit(x, axis, bit):
    other = xor_send(x, axis, bit)
    low = my_bit(axis, bit) == 0
    return jnp.stack([jnp.where(low, x, other), jnp.where(low, other, x)])


def spread_high(x, axis, low_bits):
    for bit in range(low_bits, bits_of(lax.axis_size(axis))):
        other = lax.ppermute(x, axis, [(i, i | (1 << bit)) for i in range(1 << bit)])
        x = jnp.where(my_bit(axis, bit) == 1, other, x)
    return x


def nt_dot(a, b):
    return lax.dot_general(a, b, (((1,), (1,)), ((), ())), preferred_element_type=jnp.float32)


def split(x):
    high = x.astype(jnp.bfloat16)
    return high, (x - high.astype(jnp.float32)).astype(jnp.bfloat16)


def nt_dot3(a, b):
    return nt_dot(a[0], b[0]) + (nt_dot(a[1], b[0]) + nt_dot(a[0], b[1]))


def after_kernel(x_ref, *refs):
    pass


def after(x, *others):
    return pl.pallas_call(
        after_kernel,
        out_shape=jax.ShapeDtypeStruct(x.shape, x.dtype),
        in_specs=[HBM] * (1 + len(others)),
        out_specs=HBM,
        input_output_aliases={0: 0},
        name="after",
    )(x, *others)


def pack_kernel(owner_ref, rank_ref, child_ref, first_ref, second_ref, sem):
    count = child_ref.shape[0]

    def to_first(k):
        return pltpu.make_async_copy(child_ref.at[k], first_ref.at[owner_ref[k]], sem.at[k])

    def to_second(k):
        return pltpu.make_async_copy(child_ref.at[k], second_ref.at[owner_ref[k]], sem.at[k])

    for k in range(count):
        pl.when(rank_ref[k] == 0)(lambda k=k: to_first(k).start())
        pl.when(rank_ref[k] != 0)(lambda k=k: to_second(k).start())
    for k in range(count):
        pl.when(rank_ref[k] == 0)(lambda k=k: to_first(k).wait())
        pl.when(rank_ref[k] != 0)(lambda k=k: to_second(k).wait())


def pack(owner_ids, rank, child_blocks, devices):
    count, tile, _ = child_blocks.shape
    shape = jax.ShapeDtypeStruct((devices, tile, tile), jnp.float32)
    return pl.pallas_call(
        pack_kernel,
        out_shape=(shape, shape),
        grid_spec=pltpu.PrefetchScalarGridSpec(
            num_scalar_prefetch=2,
            grid=(),
            in_specs=[WHOLE],
            out_specs=(HBM, HBM),
            scratch_shapes=[pltpu.SemaphoreType.DMA((count,))],
        ),
        compiler_params=pltpu.CompilerParams(vmem_limit_bytes=VMEM_LIMIT),
        name="pack_children",
    )(owner_ids, rank, child_blocks)


def strip_kernel(row_ref, strip_ref, got_ref, earlier_ref, out_ref, buffer, sem):
    sources = got_ref.shape[0]

    def copy(s):
        return pltpu.make_async_copy(got_ref.at[s], buffer.at[s], sem.at[s])

    for s in range(sources):
        pl.when(row_ref[s] >= 0)(lambda s=s: copy(s).start())
    out_ref[...] = strip_ref[...]
    for s in range(sources):

        @pl.when(row_ref[s] >= 0)
        def _(s=s):
            copy(s).wait()
            out_ref[row_ref[s]] = out_ref[row_ref[s]] + buffer[s]


def add_to_strip(panel_row, strip, got, earlier):
    return pl.pallas_call(
        strip_kernel,
        out_shape=jax.ShapeDtypeStruct(strip.shape, jnp.float32),
        grid_spec=pltpu.PrefetchScalarGridSpec(
            num_scalar_prefetch=1,
            grid=(),
            in_specs=[WHOLE, HBM, HBM],
            out_specs=WHOLE,
            scratch_shapes=[
                pltpu.VMEM(got.shape, jnp.float32),
                pltpu.SemaphoreType.DMA((got.shape[0],)),
            ],
        ),
        compiler_params=pltpu.CompilerParams(vmem_limit_bytes=VMEM_LIMIT),
        name="add_panel_children",
    )(panel_row, strip, got, earlier)


def exact_dot(a, b, dims):
    return lax.dot_general(a, b, (dims, ((), ())), precision=HIGHEST, preferred_element_type=jnp.float32)


def inverse_root(x):
    y = lax.rsqrt(x)
    return y * (1.5 - 0.5 * x * y * y)


def eliminate(work_ref, right_ref, t_ref, z_ref):
    n = work_ref.shape[0]
    row = lax.broadcasted_iota(jnp.int32, (n, n), 0)
    col = lax.broadcasted_iota(jnp.int32, (n, n), 1)
    right_ref[...] = jnp.where(row == col, 1.0, 0.0)
    for j in range(0, n, 2):
        lo = j // 8 * 8
        i = j - lo
        a = work_ref[lo:, :]
        z = right_ref[lo:, :]
        col0 = jnp.broadcast_to(a[:, j : j + 1], a.shape)
        col1 = jnp.broadcast_to(a[:, j + 1 : j + 2], a.shape)
        inv0 = inverse_root(col0[i : i + 1, :])
        row0 = a[i : i + 1, :] * inv0
        low0 = col0 * inv0
        cross = low0[i + 1 : i + 2, :]
        low1 = col1 - low0 * cross
        inv1 = inverse_root(low1[i + 1 : i + 2, :])
        row1 = (a[i + 1 : i + 2, :] - cross * row0) * inv1
        low1 = low1 * inv1
        z0 = z[i : i + 1, :] * inv0
        z1 = (z[i + 1 : i + 2, :] - cross * z0) * inv1
        if j + 2 < n:
            work_ref[lo:, :] = a - low0 * row0 - low1 * row1
            right_ref[lo:, :] = z - low0 * z0 - low1 * z1
        t_ref[j : j + 1, :] = row0
        t_ref[j + 1 : j + 2, :] = row1
        z_ref[j : j + 1, :] = z0
        z_ref[j + 1 : j + 2, :] = z1


def lower_of(t):
    n = t.shape[0]
    row = lax.broadcasted_iota(jnp.int32, (n, n), 0)
    col = lax.broadcasted_iota(jnp.int32, (n, n), 1)
    return jnp.where(col <= row, t.T, 0.0)


def symmetric(block):
    n = block.shape[0]
    row = lax.broadcasted_iota(jnp.int32, (n, n), 0)
    col = lax.broadcasted_iota(jnp.int32, (n, n), 1)
    return jnp.where(col <= row, block, block.T)


def factor_panel(g, scratch):
    work, right, t, z = scratch
    nt, nn = ((1,), (1,)), ((1,), (0,))
    work[...] = symmetric(g[0][0])
    eliminate(work, right, t, z)
    l00, z00 = lower_of(t[...]), z[...]
    l10 = exact_dot(g[1][0], z00, nt)
    work[...] = symmetric(g[1][1]) - exact_dot(l10, l10, nt)
    eliminate(work, right, t, z)
    l11, z11 = lower_of(t[...]), z[...]
    z10 = -exact_dot(z11, exact_dot(l10, z00, nn), nn)
    return (l00, l10, l11), (z00, z10, z11)


def store_square(ref, blocks):
    tile = blocks[0].shape[0]
    ref[:tile, :tile] = blocks[0]
    ref[:tile, tile:] = jnp.zeros((tile, tile), ref.dtype)
    ref[tile:, :tile] = blocks[1]
    ref[tile:, tile:] = blocks[2]


def leading_block(ref, i, j):
    return ref[j % 2, j // 2, i % 2, i // 2]


def panel0_kernel(corner_ref, l_ref, zh_ref, zl_ref, *scratch):
    g = [[leading_block(corner_ref, i, j) for j in range(2)] for i in range(2)]
    lower, inverse = factor_panel(g, scratch)
    store_square(l_ref, lower)
    parts = [split(block) for block in inverse]
    store_square(zh_ref, [part[0] for part in parts])
    store_square(zl_ref, [part[1] for part in parts])


def panel1_kernel(keep_ref, corner_ref, z0h_ref, z0l_ref, earlier_ref, a_ref, ah_ref, al_ref, l_ref, zh_ref, zl_ref, *scratch):
    tile = corner_ref.shape[-1]
    z0 = (z0h_ref[...], z0l_ref[...])
    rows = [jnp.concatenate([leading_block(corner_ref, 2 + i, j) for j in range(2)], axis=1) for i in range(2)]
    a = jnp.concatenate([nt_dot3(split(rows[i]), z0) * keep_ref[i].astype(jnp.float32) for i in range(2)], axis=0)
    a_ref[...] = a
    ah_ref[...], al_ref[...] = split(a)
    update = exact_dot(a, a, ((1,), (1,)))
    g = [
        [leading_block(corner_ref, 2 + i, 2 + j) - update[i * tile : (i + 1) * tile, j * tile : (j + 1) * tile] for j in range(2)]
        for i in range(2)
    ]
    lower, inverse = factor_panel(g, scratch)
    store_square(l_ref, lower)
    parts = [split(block) for block in inverse]
    store_square(zh_ref, [part[0] for part in parts])
    store_square(zl_ref, [part[1] for part in parts])


def factor_panel0(corner):
    tile = corner.shape[-1]
    full = jax.ShapeDtypeStruct((2 * tile, 2 * tile), jnp.float32)
    part = jax.ShapeDtypeStruct((2 * tile, 2 * tile), jnp.bfloat16)
    return pl.pallas_call(
        panel0_kernel,
        out_shape=(full, part, part),
        in_specs=[WHOLE],
        out_specs=(WHOLE,) * 3,
        scratch_shapes=[pltpu.VMEM((tile, tile), jnp.float32)] * 4,
        compiler_params=pltpu.CompilerParams(vmem_limit_bytes=VMEM_LIMIT),
        name="factor_panel0",
    )(corner)


def factor_panel1(corner, keep, z0, earlier):
    tile = corner.shape[-1]
    full = jax.ShapeDtypeStruct((2 * tile, 2 * tile), jnp.float32)
    part = jax.ShapeDtypeStruct((2 * tile, 2 * tile), jnp.bfloat16)
    return pl.pallas_call(
        panel1_kernel,
        out_shape=(full, part, part, full, part, part),
        grid_spec=pltpu.PrefetchScalarGridSpec(
            num_scalar_prefetch=1,
            grid=(),
            in_specs=[WHOLE] * 3 + [HBM],
            out_specs=(WHOLE,) * 6,
            scratch_shapes=[pltpu.VMEM((tile, tile), jnp.float32)] * 4,
        ),
        compiler_params=pltpu.CompilerParams(vmem_limit_bytes=VMEM_LIMIT),
        name="factor_panel1",
    )(keep, corner, *z0, earlier)


def solve_kernel(with_panel, keep0_ref, keep1_ref, place_ref, *refs):
    x_refs, factor_refs, rest = refs[:4], refs[4:10], refs[10:]
    high_ref, low_ref, xs = rest[0], rest[1], rest[-1]
    n = pl.program_id(0)
    depth, tile, _ = x_refs[0].shape
    for m in range(4):
        xs[place_ref[0] ^ m] = x_refs[m][...].reshape(depth * tile, tile)
    z0, a, z1 = [(factor_refs[2 * i][...], factor_refs[2 * i + 1][...]) for i in range(3)]

    def masked(q, keep_ref):
        return jnp.concatenate(
            [q[i * tile : (i + 1) * tile] * keep_ref[n * depth + i].astype(jnp.float32) for i in range(depth)], axis=0
        )

    x0 = jnp.concatenate([xs[0], xs[1]], axis=1)
    x1 = jnp.concatenate([xs[2], xs[3]], axis=1)
    q0 = masked(nt_dot3(split(x0), z0), keep0_ref)
    q0_parts = split(q0)
    q1 = masked(nt_dot3(split(x1 - nt_dot3(q0_parts, a)), z1), keep1_ref)
    q1_parts = split(q1)
    width = 2 * tile
    for ref, index in ((high_ref, 0), (low_ref, 1)):
        ref[:, :width] = q0_parts[index]
        ref[:, width:] = q1_parts[index]
    if with_panel:
        xs[0] = q0[:, :tile]
        xs[1] = q0[:, tile:]
        xs[2] = q1[:, :tile]
        xs[3] = q1[:, tile:]
        rest[2][...] = xs[place_ref[0]].reshape(depth, tile, tile)


def solve(strips, keep0, keep1, place, factors, with_panel):
    rows, tile, _ = strips[0].shape
    depth = rows // 2
    part = jax.ShapeDtypeStruct((rows * tile, 4 * tile), jnp.bfloat16)
    row_spec = pl.BlockSpec((depth * tile, 4 * tile), lambda n, *_: (n, 0))
    strip_spec = pl.BlockSpec((depth, tile, tile), lambda n, *_: (n, 0, 0))
    out_shape, out_specs = [part, part], [row_spec, row_spec]
    if with_panel:
        out_shape.append(jax.ShapeDtypeStruct((rows, tile, tile), jnp.float32))
        out_specs.append(strip_spec)
    return pl.pallas_call(
        functools.partial(solve_kernel, with_panel),
        out_shape=tuple(out_shape),
        grid_spec=pltpu.PrefetchScalarGridSpec(
            num_scalar_prefetch=3,
            grid=(rows // depth,),
            in_specs=[strip_spec] * 4 + [WHOLE] * 6,
            out_specs=tuple(out_specs),
            scratch_shapes=[pltpu.VMEM((4, depth * tile, tile), jnp.float32)],
        ),
        compiler_params=pltpu.CompilerParams(vmem_limit_bytes=VMEM_LIMIT),
        name="solve_rows" if with_panel else "solve_columns",
    )(keep0, keep1, place, *strips, *factors)


def final_kernel(panel_blocks, first_ref, second_ref, place_ref, front_ref, got1_ref, got2_ref, high_ref, low_ref,
                 panel_ref, l0_ref, a_ref, l1_ref, *rest):
    cols, out_ref = rest[:-1], rest[-1]
    step = pl.program_id(0)
    depth, _, bcols, _, tile, _ = front_ref.shape
    my_row, my_col, grid_rows, my_high = place_ref[0], place_ref[1], place_ref[2], place_ref[3]
    highs = len(cols) // 2
    rows = (high_ref[...], low_ref[...])
    for index in range(highs):
        col_high, col_low = cols[2 * index], cols[2 * index + 1]
        for at in range(0, bcols // highs, 2):
            piece = slice(at * tile, (at + 2) * tile)
            update = nt_dot3(rows, (col_high[piece, :], col_low[piece, :]))
            for k in range(2):
                b = (at + k) * highs + (my_high ^ index)
                for a in range(depth):
                    out_ref[a, 0, b, 0] = (
                        front_ref[a, 0, b, 0] - update[a * tile : (a + 1) * tile, k * tile : (k + 1) * tile]
                    )

    def add(list_ref, got_ref):
        def body(k, carry):
            slot = list_ref[1, k]
            a, b = slot // bcols - step * depth, slot % bcols
            out_ref[a, 0, b, 0] = out_ref[a, 0, b, 0] + got_ref[list_ref[0, k]]
            return carry

        lax.fori_loop(list_ref[2, step], list_ref[2, step + 1], body, 0)

    add(first_ref, got1_ref)
    add(second_ref, got2_ref)

    for a in range(depth):
        block_row = (step * depth + a) * grid_rows + my_row

        @pl.when(block_row < panel_blocks)
        def _(a=a):
            out_ref[a] = jnp.zeros(out_ref.shape[1:], jnp.float32)

        @pl.when(my_col < panel_blocks)
        def _(a=a):
            out_ref[a, 0, 0, 0] = panel_ref[a]

        for i in range(panel_blocks):
            for j in range(panel_blocks):

                @pl.when((block_row == i) & (my_col == j))
                def _(a=a, i=i, j=j):
                    ref = (l0_ref, None, a_ref, l1_ref)[i // 2 * 2 + j // 2]
                    rows_at, cols_at = i % 2 * tile, j % 2 * tile
                    if ref is None:
                        out_ref[a, 0, 0, 0] = jnp.zeros((tile, tile), jnp.float32)
                    else:
                        out_ref[a, 0, 0, 0] = ref[rows_at : rows_at + tile, cols_at : cols_at + tile]


def finish(depth, first, second, place, front, got1, got2, row_high, row_low, panel, corners, cols, panel_blocks):
    brows, _, bcols, _, tile, _ = front.shape
    big = pl.BlockSpec((depth, 1, bcols, 1, tile, tile), lambda i, *_: (i, 0, 0, 0, 0, 0))
    rows = pl.BlockSpec((depth * tile, row_high.shape[1]), lambda i, *_: (i, 0))
    return pl.pallas_call(
        functools.partial(final_kernel, panel_blocks),
        out_shape=jax.ShapeDtypeStruct(front.shape, jnp.float32),
        grid_spec=pltpu.PrefetchScalarGridSpec(
            num_scalar_prefetch=3,
            grid=(brows // depth,),
            in_specs=[big, WHOLE, WHOLE, rows, rows, pl.BlockSpec((depth, tile, tile), lambda i, *_: (i, 0, 0))]
            + [WHOLE] * (3 + len(cols)),
            out_specs=big,
        ),
        compiler_params=pltpu.CompilerParams(vmem_limit_bytes=VMEM_LIMIT),
        name="schur_update",
    )(first, second, place, front, got1, got2, row_high, row_low, panel, *corners, *cols)


def by_slot(slots, per_step, steps):
    count = slots.shape[0]
    index = jnp.arange(count, dtype=jnp.int32)
    key = jnp.where(slots > 0, slots, per_step * steps) * count + index
    place = jnp.sum((key[None, :] < key[:, None]).astype(jnp.int32), axis=1)
    at = place[None, :] == index[:, None]
    sources = jnp.sum(jnp.where(at, index[None, :], 0), axis=1)
    ordered = jnp.sum(jnp.where(at, slots[None, :], 0), axis=1)
    bound = jnp.minimum(index, steps) * per_step
    starts = jnp.sum(((slots > 0)[None, :] & (slots[None, :] < bound[:, None])).astype(jnp.int32), axis=1)
    return jnp.stack([sources, ordered, starts])


def local(front, child_blocks, owners, slots, pattern):
    grid_rows = lax.axis_size("prow")
    grid_cols = lax.axis_size("pcol")
    devices = grid_rows * grid_cols
    rank_r = lax.axis_index("prow")
    rank_c = lax.axis_index("pcol")
    me = rank_r * grid_cols + rank_c
    brows, _, bcols, _, tile, _ = front.shape
    row_bits, col_bits = bits_of(grid_rows), bits_of(grid_cols)
    panel_blocks = 2 * pattern.shape[0]
    panel_bits = bits_of(panel_blocks)
    owner_ids = owners[:, 0]
    children = owner_ids.shape[0]

    index = jnp.arange(children, dtype=jnp.int32)
    is_panel = (slots % bcols == 0) & (owner_ids % grid_cols < panel_blocks)
    same = owner_ids[:, None] == owner_ids[None, :]
    ahead = jnp.where(is_panel[:, None] == is_panel[None, :], index[None, :] < index[:, None], is_panel[None, :])
    rank = jnp.sum((same & ahead).astype(jnp.int32), axis=1)
    late = is_panel & (rank == 1)

    to = owner_ids[None, :] == jnp.arange(devices, dtype=jnp.int32)[:, None]
    lane = jnp.arange(tile, dtype=jnp.int32)[None, :]
    slot1 = jnp.sum(jnp.where(to & (rank == 0)[None, :], slots[None, :], 0), axis=1, keepdims=True)
    slot2 = jnp.sum(jnp.where(to & (rank == 1)[None, :], slots[None, :], 0), axis=1, keepdims=True)
    late_count = jnp.sum(late.astype(jnp.int32))
    notes = jnp.where(lane == 0, slot1, jnp.where(lane == 1, slot2, late_count))
    got_notes = lax.all_to_all(notes[:, None, :], ALL, 0, 0, tiled=True)[:, 0]

    send1, send2 = pack(owner_ids, rank, child_blocks, devices)
    got1 = lax.all_to_all(send1, ALL, 0, 0, tiled=True)

    corner = front[0, 0, 0, 0]
    corner = spread_high(corner, "prow", panel_bits)
    corner = spread_high(corner, "pcol", panel_bits)
    for bit in reversed(range(panel_bits)):
        corner = gather_bit(corner, "prow", bit)
    for bit in reversed(range(panel_bits)):
        corner = gather_bit(corner, "pcol", bit)
    l0, *z0 = factor_panel0(corner)

    first_slots, second_slots = got_notes[:, 0], got_notes[:, 1]

    def panel_here(slot):
        return (slot % bcols == 0) & (slot > 0) & (rank_c < panel_blocks)

    panel_row = jnp.where(panel_here(first_slots), first_slots // bcols, -1)
    depth = brows // 4
    lists = [by_slot(jnp.where(panel_here(s), 0, s), depth * bcols, brows // depth) for s in (first_slots, second_slots)]

    strip = front[:, 0, 0, 0]
    rounds = jnp.max(got_notes[:, 2])
    order = jnp.cumsum(late.astype(jnp.int32))

    def deliver(turn, strip):
        chosen = late & (order == turn + 1)
        block = child_blocks[jnp.argmax(chosen)]
        note = jnp.where(lane == 0, jnp.sum(jnp.where(chosen, owner_ids + 1, 0)), jnp.sum(jnp.where(chosen, slots, 0)))
        block = jnp.concatenate([block, jnp.broadcast_to(note, (8, tile)).astype(jnp.float32)], axis=0)
        for axis, bits in (("prow", row_bits), ("pcol", col_bits)):
            for bit in reversed(range(bits)):
                block = gather_bit(block, axis, bit)
        blocks = block.reshape(devices, tile + 8, tile)
        note = blocks[:, tile, :2].astype(jnp.int32)
        here = note[:, 0] == me + 1
        rows = jnp.where(here, note[:, 1] // bcols, 0)
        return strip.at[rows].add(jnp.where(here[:, None, None], blocks[:, :tile], 0.0))

    strip = lax.fori_loop(0, rounds, deliver, strip)
    strip = add_to_strip(panel_row, strip, got1, l0)
    strip = spread_high(strip, "pcol", panel_bits)

    across = xor_send(strip, "pcol", 1)
    row_strips = [strip, xor_send(strip, "pcol", 0), across, xor_send(across, "pcol", 0)]
    a, ah, al, l1, *z1 = factor_panel1(corner, pattern[0, 2:4], z0, strip)
    factors = (*z0, ah, al, *z1)
    parts = [strip]
    for bit in range(col_bits, row_bits):
        parts = parts + [after(xor_send(part, "prow", bit), l1) for part in parts]
    highs = len(parts)

    def to_columns(part, m):
        pairs = [
            ((h * grid_cols + low) * grid_cols + c, (h * grid_cols + (c ^ m)) * grid_cols + low)
            for h in range(highs)
            for low in range(grid_cols)
            for c in range(grid_cols)
        ]
        return lax.ppermute(part, ALL, pairs)

    col_strips = [[to_columns(part, m) for m in range(panel_blocks)] for part in parts]
    got2 = lax.all_to_all(after(send2, l1), ALL, 0, 0, tiled=True)

    keep0, keep1 = pattern[0], jnp.maximum(pattern[0], pattern[1])
    my_high = rank_r // grid_cols
    rows_of = jnp.arange(brows, dtype=jnp.int32) * grid_rows
    blocks = rows_of + rank_r
    row_high, row_low, panel = solve(
        row_strips, keep0[blocks], keep1[blocks], (rank_c % panel_blocks)[None], factors, True
    )
    cols = []
    for high, strips in enumerate(col_strips):
        blocks = rows_of + (my_high ^ high) * grid_cols + rank_c
        cols += solve(strips, keep0[blocks], keep1[blocks], (rank_r % panel_blocks)[None], factors, False)
    place = jnp.stack([rank_r, rank_c, jnp.int32(grid_rows), my_high])
    return finish(
        depth, *lists, place, front, got1, got2, row_high, row_low, panel, (l0, a, l1), cols, panel_blocks
    )


def solution(mesh):
    placed = (
        P(None, "prow", None, "pcol", None, None),
        P(("prow", "pcol"), None, None),
        P(("prow", "pcol"), None),
        P(("prow", "pcol")),
        P(),
    )
    return jax.shard_map(
        local,
        mesh=mesh,
        in_specs=placed,
        out_specs=P(None, "prow", None, "pcol", None, None),
        check_vma=False,
    )
```

```python
import functools

import jax
import jax.numpy as jnp
from jax import lax
from jax.experimental import pallas as pl
from jax.experimental.pallas import tpu as pltpu
from jax.sharding import PartitionSpec as P

ALL = ("prow", "pcol")
HIGHEST = lax.Precision.HIGHEST
VMEM_LIMIT = 56 * 2**20
WHOLE = pl.BlockSpec(memory_space=pltpu.VMEM)
HBM = pl.BlockSpec(memory_space=pl.ANY)


def bits_of(size):
    return size.bit_length() - 1


def xor_send(x, axis, bit):
    size = lax.axis_size(axis)
    return lax.ppermute(x, axis, [(i, i ^ (1 << bit)) for i in range(size)])


def my_bit(axis, bit):
    return (lax.axis_index(axis) >> bit) & 1


def gather_bit(x, axis, bit):
    other = xor_send(x, axis, bit)
    low = my_bit(axis, bit) == 0
    return jnp.stack([jnp.where(low, x, other), jnp.where(low, other, x)])


def spread_high(x, axis, low_bits):
    for bit in range(low_bits, bits_of(lax.axis_size(axis))):
        other = lax.ppermute(x, axis, [(i, i | (1 << bit)) for i in range(1 << bit)])
        x = jnp.where(my_bit(axis, bit) == 1, other, x)
    return x


def nt_dot(a, b):
    return lax.dot_general(a, b, (((1,), (1,)), ((), ())), preferred_element_type=jnp.float32)


def split(x):
    high = x.astype(jnp.bfloat16)
    return high, (x - high.astype(jnp.float32)).astype(jnp.bfloat16)


def nt_dot3(a, b):
    return nt_dot(a[0], b[0]) + (nt_dot(a[1], b[0]) + nt_dot(a[0], b[1]))


def after_kernel(x_ref, *refs):
    pass


def after(x, *others):
    return pl.pallas_call(
        after_kernel,
        out_shape=jax.ShapeDtypeStruct(x.shape, x.dtype),
        in_specs=[HBM] * (1 + len(others)),
        out_specs=HBM,
        input_output_aliases={0: 0},
        name="after",
    )(x, *others)


def pack_kernel(owner_ref, rank_ref, child_ref, earlier_ref, first_ref, second_ref, sem):
    count = child_ref.shape[0]

    def to_first(k):
        return pltpu.make_async_copy(child_ref.at[k], first_ref.at[owner_ref[k]], sem.at[k])

    def to_second(k):
        return pltpu.make_async_copy(child_ref.at[k], second_ref.at[owner_ref[k]], sem.at[k])

    for k in range(count):
        pl.when(rank_ref[k] == 0)(lambda k=k: to_first(k).start())
        pl.when(rank_ref[k] != 0)(lambda k=k: to_second(k).start())
    for k in range(count):
        pl.when(rank_ref[k] == 0)(lambda k=k: to_first(k).wait())
        pl.when(rank_ref[k] != 0)(lambda k=k: to_second(k).wait())


def pack(owner_ids, rank, child_blocks, devices, earlier):
    count, tile, _ = child_blocks.shape
    shape = jax.ShapeDtypeStruct((devices, tile, tile), jnp.float32)
    return pl.pallas_call(
        pack_kernel,
        out_shape=(shape, shape),
        grid_spec=pltpu.PrefetchScalarGridSpec(
            num_scalar_prefetch=2,
            grid=(),
            in_specs=[WHOLE, HBM],
            out_specs=(HBM, HBM),
            scratch_shapes=[pltpu.SemaphoreType.DMA((count,))],
        ),
        compiler_params=pltpu.CompilerParams(vmem_limit_bytes=VMEM_LIMIT),
        name="pack_children",
    )(owner_ids, rank, child_blocks, earlier)


def strip_kernel(row_ref, strip_ref, got_ref, earlier_ref, out_ref, buffer, sem):
    sources = got_ref.shape[0]

    def copy(s):
        return pltpu.make_async_copy(got_ref.at[s], buffer.at[s], sem.at[s])

    for s in range(sources):
        pl.when(row_ref[s] >= 0)(lambda s=s: copy(s).start())
    out_ref[...] = strip_ref[...]
    for s in range(sources):

        @pl.when(row_ref[s] >= 0)
        def _(s=s):
            copy(s).wait()
            out_ref[row_ref[s]] = out_ref[row_ref[s]] + buffer[s]


def add_to_strip(panel_row, strip, got, earlier):
    return pl.pallas_call(
        strip_kernel,
        out_shape=jax.ShapeDtypeStruct(strip.shape, jnp.float32),
        grid_spec=pltpu.PrefetchScalarGridSpec(
            num_scalar_prefetch=1,
            grid=(),
            in_specs=[WHOLE, HBM, HBM],
            out_specs=WHOLE,
            scratch_shapes=[
                pltpu.VMEM(got.shape, jnp.float32),
                pltpu.SemaphoreType.DMA((got.shape[0],)),
            ],
        ),
        compiler_params=pltpu.CompilerParams(vmem_limit_bytes=VMEM_LIMIT),
        name="add_panel_children",
    )(panel_row, strip, got, earlier)


def exact_dot(a, b, dims):
    return lax.dot_general(a, b, (dims, ((), ())), precision=HIGHEST, preferred_element_type=jnp.float32)


def inverse_root(x):
    y = lax.rsqrt(x)
    return y * (1.5 - 0.5 * x * y * y)


def eliminate(work_ref, right_ref, t_ref, z_ref):
    n = work_ref.shape[0]
    row = lax.broadcasted_iota(jnp.int32, (n, n), 0)
    col = lax.broadcasted_iota(jnp.int32, (n, n), 1)
    right_ref[...] = jnp.where(row == col, 1.0, 0.0)
    for j in range(0, n, 2):
        lo = j // 8 * 8
        i = j - lo
        a = work_ref[lo:, :]
        z = right_ref[lo:, :]
        col0 = jnp.broadcast_to(a[:, j : j + 1], a.shape)
        col1 = jnp.broadcast_to(a[:, j + 1 : j + 2], a.shape)
        inv0 = inverse_root(col0[i : i + 1, :])
        row0 = a[i : i + 1, :] * inv0
        low0 = col0 * inv0
        cross = low0[i + 1 : i + 2, :]
        low1 = col1 - low0 * cross
        inv1 = inverse_root(low1[i + 1 : i + 2, :])
        row1 = (a[i + 1 : i + 2, :] - cross * row0) * inv1
        low1 = low1 * inv1
        z0 = z[i : i + 1, :] * inv0
        z1 = (z[i + 1 : i + 2, :] - cross * z0) * inv1
        if j + 2 < n:
            work_ref[lo:, :] = a - low0 * row0 - low1 * row1
            right_ref[lo:, :] = z - low0 * z0 - low1 * z1
        t_ref[j : j + 1, :] = row0
        t_ref[j + 1 : j + 2, :] = row1
        z_ref[j : j + 1, :] = z0
        z_ref[j + 1 : j + 2, :] = z1


def lower_of(t):
    n = t.shape[0]
    row = lax.broadcasted_iota(jnp.int32, (n, n), 0)
    col = lax.broadcasted_iota(jnp.int32, (n, n), 1)
    return jnp.where(col <= row, t.T, 0.0)


def symmetric(block):
    n = block.shape[0]
    row = lax.broadcasted_iota(jnp.int32, (n, n), 0)
    col = lax.broadcasted_iota(jnp.int32, (n, n), 1)
    return jnp.where(col <= row, block, block.T)


def factor_panel(g, scratch):
    work, right, t, z = scratch
    nt, nn = ((1,), (1,)), ((1,), (0,))
    work[...] = symmetric(g[0][0])
    eliminate(work, right, t, z)
    l00, z00 = lower_of(t[...]), z[...]
    l10 = exact_dot(g[1][0], z00, nt)
    work[...] = symmetric(g[1][1]) - exact_dot(l10, l10, nt)
    eliminate(work, right, t, z)
    l11, z11 = lower_of(t[...]), z[...]
    z10 = -exact_dot(z11, exact_dot(l10, z00, nn), nn)
    return (l00, l10, l11), (z00, z10, z11)


def store_square(ref, blocks):
    tile = blocks[0].shape[0]
    ref[:tile, :tile] = blocks[0]
    ref[:tile, tile:] = jnp.zeros((tile, tile), ref.dtype)
    ref[tile:, :tile] = blocks[1]
    ref[tile:, tile:] = blocks[2]


def leading_block(ref, i, j):
    return ref[j % 2, j // 2, i % 2, i // 2]


def panel0_kernel(corner_ref, l_ref, zh_ref, zl_ref, *scratch):
    g = [[leading_block(corner_ref, i, j) for j in range(2)] for i in range(2)]
    lower, inverse = factor_panel(g, scratch)
    store_square(l_ref, lower)
    parts = [split(block) for block in inverse]
    store_square(zh_ref, [part[0] for part in parts])
    store_square(zl_ref, [part[1] for part in parts])


def panel1_kernel(pattern_ref, corner_ref, z0h_ref, z0l_ref, earlier_ref, a_ref, ah_ref, al_ref, l_ref, zh_ref, zl_ref, *scratch):
    tile = corner_ref.shape[-1]
    z0 = (z0h_ref[...], z0l_ref[...])
    rows = [jnp.concatenate([leading_block(corner_ref, 2 + i, j) for j in range(2)], axis=1) for i in range(2)]
    a = jnp.concatenate([nt_dot3(split(rows[i]), z0) * pattern_ref[0, 2 + i].astype(jnp.float32) for i in range(2)], axis=0)
    a_ref[...] = a
    ah_ref[...], al_ref[...] = split(a)
    update = exact_dot(a, a, ((1,), (1,)))
    g = [
        [leading_block(corner_ref, 2 + i, 2 + j) - update[i * tile : (i + 1) * tile, j * tile : (j + 1) * tile] for j in range(2)]
        for i in range(2)
    ]
    lower, inverse = factor_panel(g, scratch)
    store_square(l_ref, lower)
    parts = [split(block) for block in inverse]
    store_square(zh_ref, [part[0] for part in parts])
    store_square(zl_ref, [part[1] for part in parts])


def factor_panel0(corner):
    tile = corner.shape[-1]
    full = jax.ShapeDtypeStruct((2 * tile, 2 * tile), jnp.float32)
    part = jax.ShapeDtypeStruct((2 * tile, 2 * tile), jnp.bfloat16)
    return pl.pallas_call(
        panel0_kernel,
        out_shape=(full, part, part),
        in_specs=[WHOLE],
        out_specs=(WHOLE,) * 3,
        scratch_shapes=[pltpu.VMEM((tile, tile), jnp.float32)] * 4,
        compiler_params=pltpu.CompilerParams(vmem_limit_bytes=VMEM_LIMIT),
        name="factor_panel0",
    )(corner)


def factor_panel1(corner, pattern, z0, earlier):
    tile = corner.shape[-1]
    full = jax.ShapeDtypeStruct((2 * tile, 2 * tile), jnp.float32)
    part = jax.ShapeDtypeStruct((2 * tile, 2 * tile), jnp.bfloat16)
    return pl.pallas_call(
        panel1_kernel,
        out_shape=(full, part, part, full, part, part),
        grid_spec=pltpu.PrefetchScalarGridSpec(
            num_scalar_prefetch=1,
            grid=(),
            in_specs=[WHOLE] * 3 + [HBM],
            out_specs=(WHOLE,) * 6,
            scratch_shapes=[pltpu.VMEM((tile, tile), jnp.float32)] * 4,
        ),
        compiler_params=pltpu.CompilerParams(vmem_limit_bytes=VMEM_LIMIT),
        name="factor_panel1",
    )(pattern, corner, *z0, earlier)


def solve_kernel(with_panel, pattern_ref, place_ref, *refs):
    x_refs, factor_refs, rest = refs[:4], refs[4:10], refs[10:]
    high_ref, low_ref, xs = rest[0], rest[1], rest[-1]
    n = pl.program_id(0)
    depth, tile, _ = x_refs[0].shape
    for m in range(4):
        xs[place_ref[0] ^ m] = x_refs[m][...].reshape(depth * tile, tile)
    z0, a, z1 = [(factor_refs[2 * i][...], factor_refs[2 * i + 1][...]) for i in range(3)]

    def masked(q, panel):
        parts = []
        for i in range(depth):
            block_row = (n * depth + i) * place_ref[2] + place_ref[1]
            keep = pattern_ref[0, block_row]
            if panel == 1:
                keep = jnp.maximum(keep, pattern_ref[1, block_row])
            parts.append(q[i * tile : (i + 1) * tile] * keep.astype(jnp.float32))
        return jnp.concatenate(parts, axis=0)

    x0 = jnp.concatenate([xs[0], xs[1]], axis=1)
    x1 = jnp.concatenate([xs[2], xs[3]], axis=1)
    q0 = masked(nt_dot3(split(x0), z0), 0)
    q0_parts = split(q0)
    q1 = masked(nt_dot3(split(x1 - nt_dot3(q0_parts, a)), z1), 1)
    q1_parts = split(q1)
    width = 2 * tile
    for ref, index in ((high_ref, 0), (low_ref, 1)):
        ref[:, :width] = q0_parts[index]
        ref[:, width:] = q1_parts[index]
    if with_panel:
        xs[0] = q0[:, :tile]
        xs[1] = q0[:, tile:]
        xs[2] = q1[:, :tile]
        xs[3] = q1[:, tile:]
        rest[2][...] = xs[place_ref[0]].reshape(depth, tile, tile)


def solve(strips, pattern, place, factors, with_panel):
    rows, tile, _ = strips[0].shape
    depth = rows // 2
    part = jax.ShapeDtypeStruct((rows * tile, 4 * tile), jnp.bfloat16)
    row_spec = pl.BlockSpec((depth * tile, 4 * tile), lambda n, *_: (n, 0))
    strip_spec = pl.BlockSpec((depth, tile, tile), lambda n, *_: (n, 0, 0))
    out_shape, out_specs = [part, part], [row_spec, row_spec]
    if with_panel:
        out_shape.append(jax.ShapeDtypeStruct((rows, tile, tile), jnp.float32))
        out_specs.append(strip_spec)
    return pl.pallas_call(
        functools.partial(solve_kernel, with_panel),
        out_shape=tuple(out_shape),
        grid_spec=pltpu.PrefetchScalarGridSpec(
            num_scalar_prefetch=2,
            grid=(rows // depth,),
            in_specs=[strip_spec] * 4 + [WHOLE] * 6,
            out_specs=tuple(out_specs),
            scratch_shapes=[pltpu.VMEM((4, depth * tile, tile), jnp.float32)],
        ),
        compiler_params=pltpu.CompilerParams(vmem_limit_bytes=VMEM_LIMIT),
        name="solve_rows" if with_panel else "solve_columns",
    )(pattern, place, *strips, *factors)


def final_kernel(panel_blocks, first_ref, second_ref, place_ref, front_ref, got1_ref, got2_ref, high_ref, low_ref,
                 panel_ref, l0_ref, a_ref, l1_ref, *rest):
    cols, out_ref = rest[:-1], rest[-1]
    step = pl.program_id(0)
    depth, _, bcols, _, tile, _ = front_ref.shape
    my_row, my_col, grid_rows, my_high = place_ref[0], place_ref[1], place_ref[2], place_ref[3]
    highs = len(cols) // 2
    rows = (high_ref[...], low_ref[...])
    for index in range(highs):
        col_high, col_low = cols[2 * index], cols[2 * index + 1]
        for at in range(0, bcols // highs, 2):
            piece = slice(at * tile, (at + 2) * tile)
            update = nt_dot3(rows, (col_high[piece, :], col_low[piece, :]))
            for k in range(2):
                b = (at + k) * highs + (my_high ^ index)
                for a in range(depth):
                    out_ref[a, 0, b, 0] = (
                        front_ref[a, 0, b, 0] - update[a * tile : (a + 1) * tile, k * tile : (k + 1) * tile]
                    )

    def add(list_ref, got_ref):
        def body(k, carry):
            slot = list_ref[1, k]
            a, b = slot // bcols - step * depth, slot % bcols
            out_ref[a, 0, b, 0] = out_ref[a, 0, b, 0] + got_ref[list_ref[0, k]]
            return carry

        lax.fori_loop(list_ref[2, step], list_ref[2, step + 1], body, 0)

    add(first_ref, got1_ref)
    add(second_ref, got2_ref)

    for a in range(depth):
        block_row = (step * depth + a) * grid_rows + my_row

        @pl.when(block_row < panel_blocks)
        def _(a=a):
            out_ref[a] = jnp.zeros(out_ref.shape[1:], jnp.float32)

        @pl.when(my_col < panel_blocks)
        def _(a=a):
            out_ref[a, 0, 0, 0] = panel_ref[a]

        for i in range(panel_blocks):
            for j in range(panel_blocks):

                @pl.when((block_row == i) & (my_col == j))
                def _(a=a, i=i, j=j):
                    ref = (l0_ref, None, a_ref, l1_ref)[i // 2 * 2 + j // 2]
                    rows_at, cols_at = i % 2 * tile, j % 2 * tile
                    if ref is None:
                        out_ref[a, 0, 0, 0] = jnp.zeros((tile, tile), jnp.float32)
                    else:
                        out_ref[a, 0, 0, 0] = ref[rows_at : rows_at + tile, cols_at : cols_at + tile]


def finish(depth, first, second, place, front, got1, got2, row_high, row_low, panel, corners, cols, panel_blocks):
    brows, _, bcols, _, tile, _ = front.shape
    big = pl.BlockSpec((depth, 1, bcols, 1, tile, tile), lambda i, *_: (i, 0, 0, 0, 0, 0))
    rows = pl.BlockSpec((depth * tile, row_high.shape[1]), lambda i, *_: (i, 0))
    return pl.pallas_call(
        functools.partial(final_kernel, panel_blocks),
        out_shape=jax.ShapeDtypeStruct(front.shape, jnp.float32),
        grid_spec=pltpu.PrefetchScalarGridSpec(
            num_scalar_prefetch=3,
            grid=(brows // depth,),
            in_specs=[big, WHOLE, WHOLE, rows, rows, pl.BlockSpec((depth, tile, tile), lambda i, *_: (i, 0, 0))]
            + [WHOLE] * (3 + len(cols)),
            out_specs=big,
        ),
        compiler_params=pltpu.CompilerParams(vmem_limit_bytes=VMEM_LIMIT),
        name="schur_update",
    )(first, second, place, front, got1, got2, row_high, row_low, panel, *corners, *cols)


def by_slot(slots, per_step, steps):
    count = slots.shape[0]
    index = jnp.arange(count, dtype=jnp.int32)
    key = jnp.where(slots > 0, slots, per_step * steps) * count + index
    place = jnp.sum((key[None, :] < key[:, None]).astype(jnp.int32), axis=1)
    at = place[None, :] == index[:, None]
    sources = jnp.sum(jnp.where(at, index[None, :], 0), axis=1)
    ordered = jnp.sum(jnp.where(at, slots[None, :], 0), axis=1)
    bound = jnp.minimum(index, steps) * per_step
    starts = jnp.sum(((slots > 0)[None, :] & (slots[None, :] < bound[:, None])).astype(jnp.int32), axis=1)
    return jnp.stack([sources, ordered, starts])


def local(front, child_blocks, owners, slots, pattern):
    grid_rows = lax.axis_size("prow")
    grid_cols = lax.axis_size("pcol")
    devices = grid_rows * grid_cols
    rank_r = lax.axis_index("prow")
    rank_c = lax.axis_index("pcol")
    me = rank_r * grid_cols + rank_c
    brows, _, bcols, _, tile, _ = front.shape
    row_bits, col_bits = bits_of(grid_rows), bits_of(grid_cols)
    panel_blocks = 2 * pattern.shape[0]
    panel_bits = bits_of(panel_blocks)
    owner_ids = owners[:, 0]
    children = owner_ids.shape[0]

    corner = front[0, 0, 0, 0]
    every = jnp.stack([owner_ids, slots])
    for bit in reversed(range(panel_bits, row_bits)):
        every = gather_bit(every, "prow", bit)
    corner = spread_high(corner, "prow", panel_bits)
    first_corner = corner

    index = jnp.arange(children, dtype=jnp.int32)

    def ranked(owner, slot):
        panel = (slot % bcols == 0) & (owner % grid_cols < panel_blocks)
        same = owner[..., :, None] == owner[..., None, :]
        ahead = jnp.where(
            panel[..., :, None] == panel[..., None, :], index[None, :] < index[:, None], panel[..., None, :]
        )
        return jnp.sum((same & ahead).astype(jnp.int32), axis=-1), panel

    rank, panel = ranked(owner_ids, slots)
    late = panel & (rank == 1)
    send1, send2 = pack(owner_ids, rank, child_blocks, devices, first_corner)
    got1 = lax.all_to_all(send1, ALL, 0, 0, tiled=True)

    for bit in reversed(range(panel_bits)):
        corner = gather_bit(corner, "prow", bit)
        every = gather_bit(every, "prow", bit)
    corner = spread_high(corner, "pcol", panel_bits)
    for bit in reversed(range(panel_bits, col_bits)):
        every = gather_bit(every, "pcol", bit)
    for bit in reversed(range(panel_bits)):
        corner = gather_bit(corner, "pcol", bit)
        every = gather_bit(every, "pcol", bit)
    l0, *z0 = factor_panel0(corner)

    bits = row_bits + col_bits
    every = jnp.transpose(every, tuple(reversed(range(bits))) + (bits, bits + 1)).reshape(devices, 2, children)
    every_owner, every_slot = every[:, 0], every[:, 1]
    every_rank, every_panel = ranked(every_owner, every_slot)
    mine = every_owner == me
    trailing = jnp.where(mine & ~every_panel, every_slot, 0)
    first_slots = jnp.sum(jnp.where(every_rank == 0, trailing, 0), axis=1)
    second_slots = jnp.sum(jnp.where(every_rank == 1, trailing, 0), axis=1)
    panel_row = jnp.sum(jnp.where(mine & every_panel & (every_rank == 0), every_slot // bcols + 1, 0), axis=1) - 1
    depth = brows // 4
    lists = [by_slot(slot, depth * bcols, brows // depth) for slot in (first_slots, second_slots)]

    strip = front[:, 0, 0, 0]
    every_late = every_panel & (every_rank == 1)
    turns = jnp.cumsum(every_late.astype(jnp.int32), axis=1)
    rounds = jnp.max(turns)
    own_turns = jnp.cumsum(late.astype(jnp.int32))

    def deliver(turn, strip):
        block = child_blocks[jnp.argmax(late & (own_turns == turn + 1))]
        for axis, count in (("prow", row_bits), ("pcol", col_bits)):
            for bit in reversed(range(count)):
                block = gather_bit(block, axis, bit)
        blocks = jnp.transpose(block, tuple(reversed(range(bits))) + (bits, bits + 1)).reshape(devices, tile, tile)
        chosen = every_late & (turns == turn + 1) & mine
        rows = jnp.sum(jnp.where(chosen, every_slot // bcols, 0), axis=1)
        return strip.at[rows].add(jnp.where(jnp.any(chosen, axis=1)[:, None, None], blocks, 0.0))

    strip = lax.fori_loop(0, rounds, deliver, strip)
    strip = add_to_strip(panel_row, strip, got1, l0)
    strip = spread_high(strip, "pcol", panel_bits)

    parts = {0: strip}
    for bit in reversed(range(1, row_bits)):
        parts |= {key | (1 << bit): xor_send(part, "prow", bit) for key, part in parts.items()}
    across = xor_send(strip, "pcol", 1)
    row_strips = [strip, xor_send(strip, "pcol", 0), across, xor_send(across, "pcol", 0)]
    a, ah, al, l1, *z1 = factor_panel1(corner, pattern, z0, row_strips[1])
    factors = (*z0, ah, al, *z1)
    got2 = lax.all_to_all(after(send2, parts[1 << (row_bits - 1)]), ALL, 0, 0, tiled=True)

    def to_column(part, flip, turn):
        pairs = [
            (r * grid_cols + c, ((r & ~1) | ((c & 1) ^ turn)) * grid_cols + (((c & ~1) ^ (flip << 1)) | (r & 1)))
            for r in range(grid_rows)
            for c in range(grid_cols)
        ]
        return lax.ppermute(part, ALL, pairs)

    def wanted(high, flip):
        chosen = {key: part for key, part in parts.items() if key >> col_bits == high}
        for bit in range(1, col_bits):
            differs = my_bit("prow", bit) ^ my_bit("pcol", bit) ^ (flip if bit == 1 else 0)
            chosen = {
                key: jnp.where(differs == 1, chosen[key | (1 << bit)], part)
                for key, part in chosen.items()
                if not key >> bit & 1
            }
        (part,) = chosen.values()
        return part

    my_high = rank_r // grid_cols
    col_strips = []
    for high in range(grid_rows // grid_cols):
        sends = [wanted(high, flip) for flip in range(2)]
        col_strips.append([to_column(sends[flip], flip, turn) for flip in range(2) for turn in range(2)])
    row_place = jnp.stack([rank_c % panel_blocks, rank_r, jnp.int32(grid_rows)])
    row_high, row_low, panel = solve(row_strips, pattern, row_place, factors, True)
    cols = []
    for high, strips in enumerate(col_strips):
        base = my_bit("pcol", 1) * 2 + my_bit("prow", 0)
        col_place = jnp.stack([base, (my_high ^ high) * grid_cols + rank_c, jnp.int32(grid_rows)])
        cols += solve(strips, pattern, col_place, factors, False)
    place = jnp.stack([rank_r, rank_c, jnp.int32(grid_rows), my_high])
    return finish(
        depth, *lists, place, front, got1, got2, row_high, row_low, panel, (l0, a, l1), cols, panel_blocks
    )


def solution(mesh):
    placed = (
        P(None, "prow", None, "pcol", None, None),
        P(("prow", "pcol"), None, None),
        P(("prow", "pcol"), None),
        P(("prow", "pcol")),
        P(),
    )
    return jax.shard_map(
        local,
        mesh=mesh,
        in_specs=placed,
        out_specs=P(None, "prow", None, "pcol", None, None),
        check_vma=False,
    )
```

```python
import functools

import jax
import jax.numpy as jnp
from jax import lax
from jax.experimental import pallas as pl
from jax.experimental.pallas import tpu as pltpu
from jax.sharding import PartitionSpec as P

ALL = ("prow", "pcol")
CAP = 2
HIGHEST = lax.Precision.HIGHEST
VMEM_LIMIT = 56 * 2**20
WHOLE = pl.BlockSpec(memory_space=pltpu.VMEM)
HBM = pl.BlockSpec(memory_space=pl.ANY)


def bits_of(size):
    return size.bit_length() - 1


def xor_send(x, axis, bit):
    size = lax.axis_size(axis)
    return lax.ppermute(x, axis, [(i, i ^ (1 << bit)) for i in range(size)])


def my_bit(axis, bit):
    return (lax.axis_index(axis) >> bit) & 1


def gather_bit(x, axis, bit):
    other = xor_send(x, axis, bit)
    low = my_bit(axis, bit) == 0
    return jnp.stack([jnp.where(low, x, other), jnp.where(low, other, x)])


def spread_high(x, axis, low_bits):
    for bit in range(low_bits, bits_of(lax.axis_size(axis))):
        other = lax.ppermute(x, axis, [(i, i | (1 << bit)) for i in range(1 << bit)])
        x = jnp.where(my_bit(axis, bit) == 1, other, x)
    return x


def nt_dot(a, b):
    return lax.dot_general(a, b, (((1,), (1,)), ((), ())), preferred_element_type=jnp.float32)


def split(x):
    high = x.astype(jnp.bfloat16)
    return high, (x - high.astype(jnp.float32)).astype(jnp.bfloat16)


def nt_dot3(a, b):
    return nt_dot(a[0], b[0]) + (nt_dot(a[1], b[0]) + nt_dot(a[0], b[1]))


def after_kernel(x_ref, *refs):
    pass


def after(x, *others):
    return pl.pallas_call(
        after_kernel,
        out_shape=jax.ShapeDtypeStruct(x.shape, x.dtype),
        in_specs=[HBM] * (1 + len(others)),
        out_specs=HBM,
        input_output_aliases={0: 0},
        name="after",
    )(x, *others)


def stage(ready, work, *operands):
    shapes = jax.eval_shape(work, *operands)
    return lax.cond(
        ready, work, lambda *_: jax.tree.map(lambda part: jnp.zeros(part.shape, part.dtype), shapes), *operands
    )


def pack_kernel(place_ref, child_ref, out_ref, sem):
    count = child_ref.shape[0]

    def copy(k):
        return pltpu.make_async_copy(child_ref.at[k], out_ref.at[place_ref[k]], sem.at[k])

    for k in range(count):
        copy(k).start()
    for k in range(count):
        copy(k).wait()


def pack(place, child_blocks, places):
    count, tile, _ = child_blocks.shape
    return pl.pallas_call(
        pack_kernel,
        out_shape=jax.ShapeDtypeStruct((places, tile, tile), jnp.float32),
        grid_spec=pltpu.PrefetchScalarGridSpec(
            num_scalar_prefetch=1,
            grid=(),
            in_specs=[WHOLE],
            out_specs=HBM,
            scratch_shapes=[pltpu.SemaphoreType.DMA((count,))],
        ),
        compiler_params=pltpu.CompilerParams(vmem_limit_bytes=VMEM_LIMIT),
        name="pack_children",
    )(place, child_blocks)


def strip_kernel(row_ref, strip_ref, got_ref, out_ref, buffer, sem):
    sources = got_ref.shape[0]

    def copy(s):
        return pltpu.make_async_copy(got_ref.at[s], buffer.at[s], sem.at[s])

    for s in range(sources):
        pl.when(row_ref[s] >= 0)(lambda s=s: copy(s).start())
    out_ref[...] = strip_ref[...]
    for s in range(sources):

        @pl.when(row_ref[s] >= 0)
        def _(s=s):
            copy(s).wait()
            out_ref[row_ref[s]] = out_ref[row_ref[s]] + buffer[s]


def add_to_strip(panel_row, strip, got):
    return pl.pallas_call(
        strip_kernel,
        out_shape=jax.ShapeDtypeStruct(strip.shape, jnp.float32),
        grid_spec=pltpu.PrefetchScalarGridSpec(
            num_scalar_prefetch=1,
            grid=(),
            in_specs=[WHOLE, HBM],
            out_specs=WHOLE,
            scratch_shapes=[
                pltpu.VMEM(got.shape, jnp.float32),
                pltpu.SemaphoreType.DMA((got.shape[0],)),
            ],
        ),
        compiler_params=pltpu.CompilerParams(vmem_limit_bytes=VMEM_LIMIT),
        name="add_panel_children",
    )(panel_row, strip, got)


def exact_dot(a, b, dims):
    return lax.dot_general(a, b, (dims, ((), ())), precision=HIGHEST, preferred_element_type=jnp.float32)


def inverse_root(x):
    y = lax.rsqrt(x)
    return y * (1.5 - 0.5 * x * y * y)


def eliminate(work_ref, right_ref, t_ref, z_ref):
    n = work_ref.shape[0]
    row = lax.broadcasted_iota(jnp.int32, (n, n), 0)
    col = lax.broadcasted_iota(jnp.int32, (n, n), 1)
    right_ref[...] = jnp.where(row == col, 1.0, 0.0)
    for j in range(0, n, 2):
        lo = j // 8 * 8
        i = j - lo
        a = work_ref[lo:, :]
        z = right_ref[lo:, :]
        col0 = jnp.broadcast_to(a[:, j : j + 1], a.shape)
        col1 = jnp.broadcast_to(a[:, j + 1 : j + 2], a.shape)
        inv0 = inverse_root(col0[i : i + 1, :])
        row0 = a[i : i + 1, :] * inv0
        low0 = col0 * inv0
        cross = low0[i + 1 : i + 2, :]
        low1 = col1 - low0 * cross
        inv1 = inverse_root(low1[i + 1 : i + 2, :])
        row1 = (a[i + 1 : i + 2, :] - cross * row0) * inv1
        low1 = low1 * inv1
        z0 = z[i : i + 1, :] * inv0
        z1 = (z[i + 1 : i + 2, :] - cross * z0) * inv1
        if j + 2 < n:
            work_ref[lo:, :] = a - low0 * row0 - low1 * row1
            right_ref[lo:, :] = z - low0 * z0 - low1 * z1
        t_ref[j : j + 1, :] = row0
        t_ref[j + 1 : j + 2, :] = row1
        z_ref[j : j + 1, :] = z0
        z_ref[j + 1 : j + 2, :] = z1


def lower_of(t):
    n = t.shape[0]
    row = lax.broadcasted_iota(jnp.int32, (n, n), 0)
    col = lax.broadcasted_iota(jnp.int32, (n, n), 1)
    return jnp.where(col <= row, t.T, 0.0)


def symmetric(block):
    n = block.shape[0]
    row = lax.broadcasted_iota(jnp.int32, (n, n), 0)
    col = lax.broadcasted_iota(jnp.int32, (n, n), 1)
    return jnp.where(col <= row, block, block.T)


def factor_panel(g, scratch):
    work, right, t, z = scratch
    nt, nn = ((1,), (1,)), ((1,), (0,))
    work[...] = symmetric(g[0][0])
    eliminate(work, right, t, z)
    l00, z00 = lower_of(t[...]), z[...]
    l10 = exact_dot(g[1][0], z00, nt)
    work[...] = symmetric(g[1][1]) - exact_dot(l10, l10, nt)
    eliminate(work, right, t, z)
    l11, z11 = lower_of(t[...]), z[...]
    z10 = -exact_dot(z11, exact_dot(l10, z00, nn), nn)
    return (l00, l10, l11), (z00, z10, z11)


def store_square(ref, blocks):
    tile = blocks[0].shape[0]
    ref[:tile, :tile] = blocks[0]
    ref[:tile, tile:] = jnp.zeros((tile, tile), ref.dtype)
    ref[tile:, :tile] = blocks[1]
    ref[tile:, tile:] = blocks[2]


def leading_block(ref, i, j):
    return ref[j % 2, j // 2, i % 2, i // 2, : ref.shape[-1], :]


def panel0_kernel(corner_ref, l_ref, zh_ref, zl_ref, *scratch):
    g = [[leading_block(corner_ref, i, j) for j in range(2)] for i in range(2)]
    lower, inverse = factor_panel(g, scratch)
    store_square(l_ref, lower)
    parts = [split(block) for block in inverse]
    store_square(zh_ref, [part[0] for part in parts])
    store_square(zl_ref, [part[1] for part in parts])


def panel1_kernel(pattern_ref, corner_ref, z0h_ref, z0l_ref, a_ref, ah_ref, al_ref, l_ref, zh_ref, zl_ref, *scratch):
    tile = corner_ref.shape[-1]
    z0 = (z0h_ref[...], z0l_ref[...])
    rows = [jnp.concatenate([leading_block(corner_ref, 2 + i, j) for j in range(2)], axis=1) for i in range(2)]
    a = jnp.concatenate([nt_dot3(split(rows[i]), z0) * pattern_ref[0, 2 + i].astype(jnp.float32) for i in range(2)], axis=0)
    a_ref[...] = a
    ah_ref[...], al_ref[...] = split(a)
    update = exact_dot(a, a, ((1,), (1,)))
    g = [
        [leading_block(corner_ref, 2 + i, 2 + j) - update[i * tile : (i + 1) * tile, j * tile : (j + 1) * tile] for j in range(2)]
        for i in range(2)
    ]
    lower, inverse = factor_panel(g, scratch)
    store_square(l_ref, lower)
    parts = [split(block) for block in inverse]
    store_square(zh_ref, [part[0] for part in parts])
    store_square(zl_ref, [part[1] for part in parts])


def factor_panel0(corner):
    tile = corner.shape[-1]
    full = jax.ShapeDtypeStruct((2 * tile, 2 * tile), jnp.float32)
    part = jax.ShapeDtypeStruct((2 * tile, 2 * tile), jnp.bfloat16)
    return pl.pallas_call(
        panel0_kernel,
        out_shape=(full, part, part),
        in_specs=[WHOLE],
        out_specs=(WHOLE,) * 3,
        scratch_shapes=[pltpu.VMEM((tile, tile), jnp.float32)] * 4,
        compiler_params=pltpu.CompilerParams(vmem_limit_bytes=VMEM_LIMIT),
        name="factor_panel0",
    )(corner)


def factor_panel1(corner, pattern, z0):
    tile = corner.shape[-1]
    full = jax.ShapeDtypeStruct((2 * tile, 2 * tile), jnp.float32)
    part = jax.ShapeDtypeStruct((2 * tile, 2 * tile), jnp.bfloat16)
    return pl.pallas_call(
        panel1_kernel,
        out_shape=(full, part, part, full, part, part),
        grid_spec=pltpu.PrefetchScalarGridSpec(
            num_scalar_prefetch=1,
            grid=(),
            in_specs=[WHOLE] * 3,
            out_specs=(WHOLE,) * 6,
            scratch_shapes=[pltpu.VMEM((tile, tile), jnp.float32)] * 4,
        ),
        compiler_params=pltpu.CompilerParams(vmem_limit_bytes=VMEM_LIMIT),
        name="factor_panel1",
    )(pattern, corner, *z0)


def solve_strips(x_refs, factors, pattern_ref, first_strip, block_row_of, xs, high_ref, low_ref, size, write):
    rows, tile, _ = x_refs[0].shape
    width = 2 * tile
    z0, a, z1 = factors

    def masked(q, panel, at):
        parts = []
        for i in range(size):
            block_row = block_row_of(at + i)
            keep = pattern_ref[0, block_row]
            if panel == 1:
                keep = jnp.maximum(keep, pattern_ref[1, block_row])
            parts.append(q[i * tile : (i + 1) * tile] * keep.astype(jnp.float32))
        return jnp.concatenate(parts, axis=0)

    for at in range(0, rows, size):
        for m in range(4):
            xs[first_strip ^ m] = x_refs[m][at : at + size].reshape(size * tile, tile)
        x0 = jnp.concatenate([xs[0], xs[1]], axis=1)
        x1 = jnp.concatenate([xs[2], xs[3]], axis=1)
        q0 = masked(nt_dot3(split(x0), z0), 0, at)
        q0_parts = split(q0)
        q1 = masked(nt_dot3(split(x1 - nt_dot3(q0_parts, a)), z1), 1, at)
        q1_parts = split(q1)
        where = slice(at * tile, (at + size) * tile)
        for ref, index in ((high_ref, 0), (low_ref, 1)):
            ref[where, :width] = q0_parts[index]
            ref[where, width:] = q1_parts[index]
        if write is not None:
            for index, q in enumerate((q0, q1)):
                xs[2 * index] = q[:, :tile]
                xs[2 * index + 1] = q[:, tile:]
            write(at)


def factor_pairs(refs):
    return [(refs[2 * i][...], refs[2 * i + 1][...]) for i in range(3)]


def rows_kernel(size, pattern_ref, place_ref, *refs):
    x_refs, factor_refs, (high_ref, low_ref, panel_ref, xs) = refs[:4], refs[4:10], refs[10:]
    tile = x_refs[0].shape[-1]
    strip = place_ref[1] % 4

    def write(at):
        panel_ref[at : at + size] = xs[strip].reshape(size, tile, tile)

    def block_row_of(a):
        return a * place_ref[2] + place_ref[0]

    solve_strips(x_refs, factor_pairs(factor_refs), pattern_ref, strip, block_row_of, xs, high_ref, low_ref, size, write)


def solve_rows(strips, pattern, place, factors):
    rows, tile, _ = strips[0].shape
    size = min(rows, 4)
    part = jax.ShapeDtypeStruct((rows * tile, 4 * tile), jnp.bfloat16)
    return pl.pallas_call(
        functools.partial(rows_kernel, size),
        out_shape=(part, part, jax.ShapeDtypeStruct((rows, tile, tile), jnp.float32)),
        grid_spec=pltpu.PrefetchScalarGridSpec(
            num_scalar_prefetch=2,
            grid=(),
            in_specs=[WHOLE] * 10,
            out_specs=(WHOLE,) * 3,
            scratch_shapes=[pltpu.VMEM((4, size * tile, tile), jnp.float32)],
        ),
        compiler_params=pltpu.CompilerParams(vmem_limit_bytes=VMEM_LIMIT),
        name="solve_rows",
    )(pattern, place, *strips, *factors)


def schur_kernel(size, panel_blocks, list_ref, pattern_ref, place_ref, before_ref, front_ref, got_ref, high_ref, low_ref,
                 panel_ref, l0_ref, a_ref, l1_ref, *refs):
    x_refs, factor_refs, (out_ref, xs, col_high, col_low) = refs[:4], refs[4:10], refs[10:]
    step = pl.program_id(0)
    depth, bcols, _, tile, _ = front_ref.shape
    my_row, my_col, grid_rows, grid_cols, share = [place_ref[i] for i in range(5)]

    @pl.when(step == 0)
    def _():
        def block_row_of(a):
            return a * grid_rows + share * grid_cols + my_col

        solve_strips(
            x_refs, factor_pairs(factor_refs), pattern_ref, my_row % 4, block_row_of, xs, col_high, col_low, size, None
        )

    rows = (high_ref[...], low_ref[...])
    for at in range(0, bcols, 2):
        piece = slice(at * tile, (at + 2) * tile)
        update = nt_dot3(rows, (col_high[piece, :], col_low[piece, :]))
        for k in range(2):
            for a in range(depth):
                out_ref[a, at + k, 0] = (
                    front_ref[a, at + k, 0] - update[a * tile : (a + 1) * tile, k * tile : (k + 1) * tile]
                )

    def body(k, carry):
        slot = list_ref[1, k]
        a, b = slot // bcols - step * depth, slot % bcols
        out_ref[a, b, 0] = out_ref[a, b, 0] + got_ref[list_ref[0, k]]
        return carry

    lax.fori_loop(list_ref[2, step], list_ref[2, step + 1], body, 0)

    for a in range(depth):
        block_row = (step * depth + a) * grid_rows + my_row

        @pl.when(block_row < panel_blocks)
        def _(a=a):
            out_ref[a] = jnp.zeros(out_ref.shape[1:], jnp.float32)

        @pl.when((my_col < panel_blocks) & (share == 0))
        def _(a=a):
            out_ref[a, 0, 0] = panel_ref[a]

        for i in range(panel_blocks):
            for j in range(panel_blocks):

                @pl.when((block_row == i) & (my_col == j) & (share == 0))
                def _(a=a, i=i, j=j):
                    ref = (l0_ref, None, a_ref, l1_ref)[i // 2 * 2 + j // 2]
                    rows_at, cols_at = i % 2 * tile, j % 2 * tile
                    if ref is None:
                        out_ref[a, 0, 0] = jnp.zeros((tile, tile), jnp.float32)
                    else:
                        out_ref[a, 0, 0] = ref[rows_at : rows_at + tile, cols_at : cols_at + tile]


def schur_share(depth, listed, pattern, place, before, front, got, rows, panel, corners, strips, factors, panel_blocks):
    brows, bcols, _, tile, _ = front.shape
    size = min(brows, 4)
    width = 4 * tile
    share = pl.BlockSpec((depth, bcols, 1, tile, tile), lambda i, listed, pattern, place: (i, 0, place[4], 0, 0))
    row_spec = pl.BlockSpec((depth * tile, width), lambda i, *_: (i, 0))
    return pl.pallas_call(
        functools.partial(schur_kernel, size, panel_blocks),
        out_shape=jax.ShapeDtypeStruct(front.shape, jnp.float32),
        grid_spec=pltpu.PrefetchScalarGridSpec(
            num_scalar_prefetch=3,
            grid=(brows // depth,),
            in_specs=[HBM, share, WHOLE, row_spec, row_spec, pl.BlockSpec((depth, tile, tile), lambda i, *_: (i, 0, 0))]
            + [WHOLE] * 13,
            out_specs=share,
            scratch_shapes=[
                pltpu.VMEM((4, size * tile, tile), jnp.float32),
                pltpu.VMEM((brows * tile, width), jnp.bfloat16),
                pltpu.VMEM((brows * tile, width), jnp.bfloat16),
            ],
        ),
        input_output_aliases={3: 0} if before is not front else {},
        compiler_params=pltpu.CompilerParams(vmem_limit_bytes=VMEM_LIMIT),
        name="schur_share",
    )(listed, pattern, place, before, front, got, *rows, panel, *corners, *strips, *factors)


def in_slot_order(slots, valid):
    count = slots.shape[0]
    index = jnp.arange(count, dtype=jnp.int32)
    key = jnp.where(valid, slots, 2**20) * count + index
    place = jnp.sum((key[None, :] < key[:, None]).astype(jnp.int32), axis=1)
    at = place[None, :] == index[:, None]
    return jnp.sum(jnp.where(at, index[None, :], 0), axis=1), jnp.sum(jnp.where(at, slots[None, :], 0), axis=1)


def by_slot(slots, valid, per_step, steps):
    index = jnp.arange(slots.shape[0], dtype=jnp.int32)
    sources, ordered = in_slot_order(slots, valid)
    bound = jnp.minimum(index, steps) * per_step
    starts = jnp.sum((valid[None, :] & (slots[None, :] < bound[:, None])).astype(jnp.int32), axis=1)
    return jnp.stack([sources, ordered, starts])


def local(front, child_blocks, owners, slots, pattern):
    grid_rows = lax.axis_size("prow")
    grid_cols = lax.axis_size("pcol")
    devices = grid_rows * grid_cols
    rank_r = lax.axis_index("prow")
    rank_c = lax.axis_index("pcol")
    me = rank_r * grid_cols + rank_c
    brows, _, bcols, _, tile, _ = front.shape
    row_bits, col_bits = bits_of(grid_rows), bits_of(grid_cols)
    panel_blocks = 2 * pattern.shape[0]
    panel_bits = bits_of(panel_blocks)
    owner_ids = owners[:, 0]
    children = owner_ids.shape[0]

    notes = jnp.zeros((8, tile), jnp.float32)
    notes = notes.at[0, :children].set(owner_ids.astype(jnp.float32)).at[1, :children].set(slots.astype(jnp.float32))
    corner = front[0, 0, 0, 0]

    def spread(corner, notes, axis):
        for bit in range(panel_bits, bits_of(lax.axis_size(axis))):
            other = xor_send(jnp.concatenate([corner, notes], axis=-2), axis, bit)
            high = my_bit(axis, bit) == 1
            corner, others = jnp.where(high, other[..., : corner.shape[-2], :], corner), other[..., corner.shape[-2] :, :]
            notes = jnp.concatenate([jnp.where(high, others, notes), jnp.where(high, notes, others)], axis=-2)
        return corner, notes

    index = jnp.arange(children, dtype=jnp.int32)

    def ranked(owner):
        same = owner[..., :, None] == owner[..., None, :]
        return jnp.sum((same & (index[None, :] < index[:, None])).astype(jnp.int32), axis=-1)

    corner, notes = spread(corner, notes, "prow")
    corner = jnp.concatenate([corner, notes], axis=0)
    for bit in reversed(range(1, panel_bits)):
        corner = gather_bit(corner, "prow", bit)
    send = after(pack(owner_ids * CAP + ranked(owner_ids), child_blocks, devices * CAP), corner)
    got = lax.all_to_all(send, ALL, 0, 0, tiled=True)
    corner = after(corner, send)
    depth = brows // 4
    highs = grid_rows // grid_cols
    my_high = rank_r // grid_cols
    share_cols = bcols // highs
    shares = [my_high ^ high for high in range(highs)]
    ready = owner_ids[0] >= 0

    def beside_children(corner):
        corner = gather_bit(corner, "prow", 0)
        corner, notes = spread(corner[..., :tile, :], corner[..., tile:, :], "pcol")
        corner = jnp.concatenate([corner, notes], axis=-2)
        for bit in reversed(range(panel_bits)):
            corner = gather_bit(corner, "pcol", bit)
        l0, *z0 = factor_panel0(corner)
        a, ah, al, l1, *z1 = factor_panel1(corner, pattern, z0)

        bits = row_bits + col_bits
        noted = corner[..., tile:, :].reshape((2,) * bits + (8, tile))[..., :2, :children].astype(jnp.int32)
        dims = [("col", bit) for bit in range(panel_bits)] + [("row", bit) for bit in range(panel_bits)]
        dims += [("col", bit) for bit in reversed(range(panel_bits, col_bits))]
        dims += [("row", bit) for bit in reversed(range(panel_bits, row_bits))]
        linear = [("row", bit) for bit in reversed(range(row_bits))] + [("col", bit) for bit in reversed(range(col_bits))]
        every = jnp.transpose(noted, [dims.index(dim) for dim in linear] + [bits, bits + 1])
        every = every.reshape(devices, 2, children)
        every_owner, every_slot = every[:, 0], every[:, 1]
        every_rank = ranked(every_owner)
        mine = every_owner == me
        got_slots = jnp.stack(
            [jnp.sum(jnp.where(mine & (every_rank == rank), every_slot, 0), axis=1) for rank in range(CAP)], axis=1
        ).reshape(-1)
        panel_here = (got_slots > 0) & (got_slots % bcols == 0) & (rank_c < panel_blocks)
        panel_row = jnp.where(panel_here, got_slots // bcols, -1)

        def listed(share):
            inside = (got_slots > 0) & ~panel_here & (got_slots % bcols % highs == share)
            slot = got_slots // bcols * share_cols + got_slots % bcols // highs
            return by_slot(slot, inside, depth * share_cols, brows // depth)

        return (l0, a, l1), (*z0, ah, al, *z1), panel_row, [listed(share) for share in shares]

    corners, factors, panel_row, lists = stage(ready, beside_children, corner)
    strip = add_to_strip(panel_row, front[:, 0, 0, 0], got)
    strip = spread_high(strip, "pcol", panel_bits)

    def to_column(part, m):
        pairs = [
            ((high * grid_cols + low) * grid_cols + c, (high * grid_cols + (c ^ m)) * grid_cols + low)
            for high in range(highs)
            for low in range(grid_cols)
            for c in range(grid_cols)
        ]
        return lax.ppermute(part, ALL, pairs)

    parts = {0: strip}
    for bit in reversed(range(col_bits, row_bits)):
        parts |= {key | (1 << (bit - col_bits)): xor_send(part, "prow", bit) for key, part in parts.items()}
    col_strips = [[to_column(parts[high], m) for m in range(panel_blocks)] for high in range(highs)]
    across, beside = xor_send(strip, "pcol", 1), xor_send(strip, "pcol", 0)
    row_strips = [strip, beside, across, xor_send(across, "pcol", 0)]
    place = jnp.stack([rank_r, rank_c, jnp.int32(grid_rows)])
    row_high, row_low, panel = solve_rows(row_strips, pattern, place, factors)
    blocks = front.reshape(brows, share_cols, highs, tile, tile)
    out = blocks
    for high, strips in enumerate(col_strips):
        place = jnp.stack([rank_r, rank_c, jnp.int32(grid_rows), jnp.int32(grid_cols), shares[high]])
        out = schur_share(
            depth, lists[high], pattern, place, out, blocks, got, (row_high, row_low), panel, corners, strips, factors,
            panel_blocks,
        )
    return out.reshape(front.shape)


def solution(mesh):
    placed = (
        P(None, "prow", None, "pcol", None, None),
        P(("prow", "pcol"), None, None),
        P(("prow", "pcol"), None),
        P(("prow", "pcol")),
        P(),
    )
    return jax.shard_map(
        local,
        mesh=mesh,
        in_specs=placed,
        out_specs=P(None, "prow", None, "pcol", None, None),
        check_vma=False,
    )
```

```python
import functools

import jax
import jax.numpy as jnp
from jax import lax
from jax.experimental import pallas as pl
from jax.experimental.pallas import tpu as pltpu
from jax.sharding import PartitionSpec as P

ALL = ("prow", "pcol")
CAP = 2
DEPTH = 2
HIGHEST = lax.Precision.HIGHEST
WHOLE = pl.BlockSpec(memory_space=pltpu.VMEM)
HBM = pl.BlockSpec(memory_space=pltpu.HBM)
ANY = pl.BlockSpec(memory_space=pl.ANY)


def vmem(mib, *arrays):
    held = sum(array.size * array.dtype.itemsize for array in arrays)
    return pltpu.CompilerParams(vmem_limit_bytes=mib * 2**20 + held)


def bits_of(size):
    return size.bit_length() - 1


def xor_send(x, axis, bit):
    size = lax.axis_size(axis)
    return lax.ppermute(x, axis, [(i, i ^ (1 << bit)) for i in range(size)])


def my_bit(axis, bit):
    return (lax.axis_index(axis) >> bit) & 1


def gather_bit(x, axis, bit):
    other = xor_send(x, axis, bit)
    low = my_bit(axis, bit) == 0
    return jnp.stack([jnp.where(low, x, other), jnp.where(low, other, x)])


def gather_bits(x, axis, bits):
    size = lax.axis_size(axis)
    masks = [0]
    for bit in bits:
        masks = [mask | on for mask in masks for on in (0, 1 << bit)]
    sent = [lax.ppermute(x, axis, [(i, i ^ mask) for i in range(size)]) if mask else x for mask in masks]
    whole = jnp.stack(sent).reshape((2,) * len(bits) + x.shape)
    for dim, bit in enumerate(bits):
        whole = jnp.where(my_bit(axis, bit) == 0, whole, jnp.flip(whole, dim))
    return whole


def spread_high(x, axis, low_bits):
    for bit in range(low_bits, bits_of(lax.axis_size(axis))):
        other = lax.ppermute(x, axis, [(i, i | (1 << bit)) for i in range(1 << bit)])
        x = jnp.where(my_bit(axis, bit) == 1, other, x)
    return x


def nt_dot(a, b):
    return lax.dot_general(a, b, (((1,), (1,)), ((), ())), preferred_element_type=jnp.float32)


def split(x):
    high = x.astype(jnp.bfloat16)
    return high, (x - high.astype(jnp.float32)).astype(jnp.bfloat16)


def nt_dot3(a, b):
    return nt_dot(a[0], b[0]) + (nt_dot(a[1], b[0]) + nt_dot(a[0], b[1]))


def after_kernel(x_ref, *refs):
    pass


def after(x, *others):
    return pl.pallas_call(
        after_kernel,
        out_shape=jax.ShapeDtypeStruct(x.shape, x.dtype),
        in_specs=[ANY] * (1 + len(others)),
        out_specs=ANY,
        input_output_aliases={0: 0},
        name="after",
    )(x, *others)


def stage(ready, work, *operands):
    shapes = jax.eval_shape(work, *operands)
    return lax.cond(
        ready, work, lambda *_: jax.tree.map(lambda part: jnp.zeros(part.shape, part.dtype), shapes), *operands
    )


def pack_kernel(place_ref, child_ref, out_ref, sem):
    count = child_ref.shape[0]

    def copy(k):
        return pltpu.make_async_copy(child_ref.at[k], out_ref.at[place_ref[k]], sem.at[k])

    for k in range(count):
        copy(k).start()
    for k in range(count):
        copy(k).wait()


def pack(place, child_blocks, places):
    count, tile, _ = child_blocks.shape
    return pl.pallas_call(
        pack_kernel,
        out_shape=jax.ShapeDtypeStruct((places, tile, tile), jnp.float32),
        grid_spec=pltpu.PrefetchScalarGridSpec(
            num_scalar_prefetch=1,
            grid=(),
            in_specs=[WHOLE],
            out_specs=HBM,
            scratch_shapes=[pltpu.SemaphoreType.DMA((count,))],
        ),
        compiler_params=vmem(48, child_blocks),
        name="pack_children",
    )(place, child_blocks)


def strip_kernel(row_ref, strip_ref, got_ref, out_ref, buffer, sem):
    sources = got_ref.shape[0]

    def copy(s):
        return pltpu.make_async_copy(got_ref.at[s], buffer.at[s], sem.at[s])

    for s in range(sources):
        pl.when(row_ref[s] >= 0)(lambda s=s: copy(s).start())
    out_ref[...] = strip_ref[...]
    for s in range(sources):

        @pl.when(row_ref[s] >= 0)
        def _(s=s):
            copy(s).wait()
            out_ref[row_ref[s]] = out_ref[row_ref[s]] + buffer[s]


def add_to_strip(panel_row, strip, got):
    return pl.pallas_call(
        strip_kernel,
        out_shape=jax.ShapeDtypeStruct(strip.shape, jnp.float32),
        grid_spec=pltpu.PrefetchScalarGridSpec(
            num_scalar_prefetch=1,
            grid=(),
            in_specs=[WHOLE, HBM],
            out_specs=WHOLE,
            scratch_shapes=[
                pltpu.VMEM(got.shape, jnp.float32),
                pltpu.SemaphoreType.DMA((got.shape[0],)),
            ],
        ),
        compiler_params=vmem(8, got),
        name="add_panel_children",
    )(panel_row, strip, got)


def exact_dot(a, b, dims):
    return lax.dot_general(a, b, (dims, ((), ())), precision=HIGHEST, preferred_element_type=jnp.float32)


def inverse_root(x):
    y = lax.rsqrt(x)
    return y * (1.5 - 0.5 * x * y * y)


def eliminate(work_ref, right_ref, t_ref, z_ref):
    n = work_ref.shape[0]
    row = lax.broadcasted_iota(jnp.int32, (n, n), 0)
    col = lax.broadcasted_iota(jnp.int32, (n, n), 1)
    right_ref[...] = jnp.where(row == col, 1.0, 0.0)
    for j in range(0, n, 2):
        lo = j // 8 * 8
        i = j - lo
        a = work_ref[lo:, :]
        z = right_ref[lo:, :]
        col0 = jnp.broadcast_to(a[:, j : j + 1], a.shape)
        col1 = jnp.broadcast_to(a[:, j + 1 : j + 2], a.shape)
        inv0 = inverse_root(col0[i : i + 1, :])
        row0 = a[i : i + 1, :] * inv0
        low0 = col0 * inv0
        cross = low0[i + 1 : i + 2, :]
        low1 = col1 - low0 * cross
        inv1 = inverse_root(low1[i + 1 : i + 2, :])
        row1 = (a[i + 1 : i + 2, :] - cross * row0) * inv1
        low1 = low1 * inv1
        z0 = z[i : i + 1, :] * inv0
        z1 = (z[i + 1 : i + 2, :] - cross * z0) * inv1
        if j + 2 < n:
            work_ref[lo:, :] = a - low0 * row0 - low1 * row1
            right_ref[lo:, :] = z - low0 * z0 - low1 * z1
        t_ref[j : j + 1, :] = row0
        t_ref[j + 1 : j + 2, :] = row1
        z_ref[j : j + 1, :] = z0
        z_ref[j + 1 : j + 2, :] = z1


def lower_of(t):
    n = t.shape[0]
    row = lax.broadcasted_iota(jnp.int32, (n, n), 0)
    col = lax.broadcasted_iota(jnp.int32, (n, n), 1)
    return jnp.where(col <= row, t.T, 0.0)


def symmetric(block):
    n = block.shape[0]
    row = lax.broadcasted_iota(jnp.int32, (n, n), 0)
    col = lax.broadcasted_iota(jnp.int32, (n, n), 1)
    return jnp.where(col <= row, block, block.T)


def factor_panel(g, scratch):
    work, right, t, z = scratch
    nt, nn = ((1,), (1,)), ((1,), (0,))
    work[...] = symmetric(g[0][0])
    eliminate(work, right, t, z)
    l00, z00 = lower_of(t[...]), z[...]
    l10 = exact_dot(g[1][0], z00, nt)
    work[...] = symmetric(g[1][1]) - exact_dot(l10, l10, nt)
    eliminate(work, right, t, z)
    l11, z11 = lower_of(t[...]), z[...]
    z10 = -exact_dot(z11, exact_dot(l10, z00, nn), nn)
    return (l00, l10, l11), (z00, z10, z11)


def store_square(ref, blocks):
    tile = blocks[0].shape[0]
    ref[:tile, :tile] = blocks[0]
    ref[:tile, tile:] = jnp.zeros((tile, tile), ref.dtype)
    ref[tile:, :tile] = blocks[1]
    ref[tile:, tile:] = blocks[2]


def leading_block(ref, i, j):
    return ref[j % 2, j // 2, i % 2, i // 2, : ref.shape[-1], :]


def panel0_kernel(corner_ref, l_ref, zh_ref, zl_ref, *scratch):
    g = [[leading_block(corner_ref, i, j) for j in range(2)] for i in range(2)]
    lower, inverse = factor_panel(g, scratch)
    store_square(l_ref, lower)
    parts = [split(block) for block in inverse]
    store_square(zh_ref, [part[0] for part in parts])
    store_square(zl_ref, [part[1] for part in parts])


def panel1_kernel(pattern_ref, corner_ref, z0h_ref, z0l_ref, a_ref, ah_ref, al_ref, l_ref, zh_ref, zl_ref, *scratch):
    tile = corner_ref.shape[-1]
    z0 = (z0h_ref[...], z0l_ref[...])
    rows = [jnp.concatenate([leading_block(corner_ref, 2 + i, j) for j in range(2)], axis=1) for i in range(2)]
    a = jnp.concatenate([nt_dot3(split(rows[i]), z0) * pattern_ref[0, 2 + i].astype(jnp.float32) for i in range(2)], axis=0)
    a_ref[...] = a
    ah_ref[...], al_ref[...] = split(a)
    update = exact_dot(a, a, ((1,), (1,)))
    g = [
        [leading_block(corner_ref, 2 + i, 2 + j) - update[i * tile : (i + 1) * tile, j * tile : (j + 1) * tile] for j in range(2)]
        for i in range(2)
    ]
    lower, inverse = factor_panel(g, scratch)
    store_square(l_ref, lower)
    parts = [split(block) for block in inverse]
    store_square(zh_ref, [part[0] for part in parts])
    store_square(zl_ref, [part[1] for part in parts])


def factor_panel0(corner):
    tile = corner.shape[-1]
    full = jax.ShapeDtypeStruct((2 * tile, 2 * tile), jnp.float32)
    part = jax.ShapeDtypeStruct((2 * tile, 2 * tile), jnp.bfloat16)
    return pl.pallas_call(
        panel0_kernel,
        out_shape=(full, part, part),
        in_specs=[WHOLE],
        out_specs=(WHOLE,) * 3,
        scratch_shapes=[pltpu.VMEM((tile, tile), jnp.float32)] * 4,
        compiler_params=vmem(12),
        name="factor_panel0",
    )(corner)


def factor_panel1(corner, pattern, z0):
    tile = corner.shape[-1]
    full = jax.ShapeDtypeStruct((2 * tile, 2 * tile), jnp.float32)
    part = jax.ShapeDtypeStruct((2 * tile, 2 * tile), jnp.bfloat16)
    return pl.pallas_call(
        panel1_kernel,
        out_shape=(full, part, part, full, part, part),
        grid_spec=pltpu.PrefetchScalarGridSpec(
            num_scalar_prefetch=1,
            grid=(),
            in_specs=[WHOLE] * 3,
            out_specs=(WHOLE,) * 6,
            scratch_shapes=[pltpu.VMEM((tile, tile), jnp.float32)] * 4,
        ),
        compiler_params=vmem(12),
        name="factor_panel1",
    )(pattern, corner, *z0)


def nn_dot3(a, b):
    def dot(x, y):
        return lax.dot_general(x, y, (((1,), (0,)), ((), ())), preferred_element_type=jnp.float32)

    return dot(a[0], b[0]) + (dot(a[1], b[0]) + dot(a[0], b[1]))


def rows_kernel(size, pattern_ref, place_ref, *refs):
    strip_refs, factor_refs, (high_ref, low_ref, panel_ref, xs, x_refs, sem) = refs[:4], refs[4:10], refs[10:]
    _, rows, tile, _ = x_refs.shape
    copies = [pltpu.make_async_copy(ref, x_refs.at[m], sem.at[m]) for m, ref in enumerate(strip_refs)]
    for copy in copies:
        copy.start()
    for copy in copies:
        copy.wait()
    z0, a, z1 = [(factor_refs[2 * i][...], factor_refs[2 * i + 1][...]) for i in range(3)]
    strip, base = place_ref[1] % 4, place_ref[0] % 4

    def masked(q, panel, at):
        parts = []
        for i in range(size):
            block_row = (at + i) * place_ref[2] + place_ref[0]
            keep = pattern_ref[0, block_row]
            if panel == 1:
                keep = jnp.maximum(keep, pattern_ref[1, block_row])
            parts.append(q[i * tile : (i + 1) * tile] * keep.astype(jnp.float32))
        return jnp.concatenate(parts, axis=0)

    def spread_out(first, second):
        for index, whole in enumerate((first, second)):
            xs[2 * index] = whole[:, :tile]
            xs[2 * index + 1] = whole[:, tile:]

    for at in range(0, rows, size):
        for m in range(4):
            xs[strip ^ m] = x_refs[m, at : at + size].reshape(size * tile, tile)
        x0 = jnp.concatenate([xs[0], xs[1]], axis=1)
        x1 = jnp.concatenate([xs[2], xs[3]], axis=1)
        q0 = masked(nt_dot3(split(x0), z0), 0, at)
        q0_parts = split(q0)
        q1 = masked(nt_dot3(split(x1 - nt_dot3(q0_parts, a)), z1), 1, at)
        spread_out(q0, q1)
        panel_ref[at : at + size] = xs[strip].reshape(size, tile, tile)
        w1 = nn_dot3(split(q1), z1)
        w0 = nn_dot3(split(q0 - nn_dot3(split(w1), a)), z0)
        spread_out(w0, w1)
        for m in range(4):
            high_ref[at * tile : (at + size) * tile, m * tile : (m + 1) * tile], low_ref[
                at * tile : (at + size) * tile, m * tile : (m + 1) * tile
            ] = split(xs[base ^ m])


def solve_rows(strips, pattern, place, factors):
    rows, tile, _ = strips[0].shape
    size = min(rows, 4)
    part = jax.ShapeDtypeStruct((rows * tile, 4 * tile), jnp.bfloat16)
    return pl.pallas_call(
        functools.partial(rows_kernel, size),
        out_shape=(part, part, jax.ShapeDtypeStruct((rows, tile, tile), jnp.float32)),
        grid_spec=pltpu.PrefetchScalarGridSpec(
            num_scalar_prefetch=2,
            grid=(),
            in_specs=[ANY] * 4 + [WHOLE] * 6,
            out_specs=(WHOLE,) * 3,
            scratch_shapes=[
                pltpu.VMEM((4, size * tile, tile), jnp.float32),
                pltpu.VMEM((4, rows, tile, tile), jnp.float32),
                pltpu.SemaphoreType.DMA((4,)),
            ],
        ),
        compiler_params=vmem(20),
        name="solve_rows",
    )(pattern, place, *strips, *factors)


def schur_kernel(panel_blocks, list_ref, pattern_ref, place_ref, before_ref, front_ref, got_ref, high_ref, low_ref,
                 panel_ref, l0_ref, a_ref, l1_ref, *refs):
    strip_refs, (out_ref, col_high, col_low, blocks, x_refs, children, child_sem, read_sem, write_sem, x_sem) = refs[:5], refs[5:]
    brows, bcols, tile, _ = blocks.shape
    steps = brows // DEPTH
    my_row, my_col, grid_rows, grid_cols, share = [place_ref[i] for i in range(5)]

    def child(k):
        return pltpu.make_async_copy(got_ref.at[list_ref[0, k]], children.at[k], child_sem.at[k])

    def read(step):
        rows = pl.ds(step * DEPTH, DEPTH)
        return pltpu.make_async_copy(front_ref.at[rows, :, share], blocks.at[rows], read_sem.at[step])

    def write(step):
        rows = pl.ds(step * DEPTH, DEPTH)
        return pltpu.make_async_copy(blocks.at[rows], out_ref.at[rows, :, share], write_sem.at[step])

    own = my_row % grid_cols == my_col

    def strip(m, source):
        return pltpu.make_async_copy(strip_refs[source], x_refs.at[m], x_sem.at[m])

    pl.when(own)(lambda: strip(0, 4).start())
    pl.when(jnp.logical_not(own))(lambda: strip(0, 0).start())
    for m in range(1, 4):
        strip(m, m).start()
    for step in range(steps):
        read(step).start()

    def start(k, carry):
        child(k).start()
        return carry

    lax.fori_loop(0, list_ref[2, steps], start, 0)

    for m in range(4):
        strip(m, m).wait()
        for a in range(bcols):
            block_row = a * grid_rows + share * grid_cols + my_col
            first_keep = pattern_ref[0, block_row]
            keep = jnp.where((my_row ^ m) & 2 == 0, first_keep, jnp.maximum(first_keep, pattern_ref[1, block_row]))
            high, low = split(x_refs[m, a] * keep.astype(jnp.float32))
            at = (slice(a * tile, (a + 1) * tile), slice(m * tile, (m + 1) * tile))
            col_high[at] = high
            col_low[at] = low
    for step in range(steps):
        first = step * DEPTH
        rows = tuple(ref[first * tile : (first + DEPTH) * tile, :] for ref in (high_ref, low_ref))
        read(step).wait()
        for at in range(0, bcols, 2):
            cols = slice(at * tile, (at + 2) * tile)
            update = nt_dot3(rows, (col_high[cols, :], col_low[cols, :]))
            for k in range(2):
                for a in range(DEPTH):
                    blocks[first + a, at + k] = (
                        blocks[first + a, at + k] - update[a * tile : (a + 1) * tile, k * tile : (k + 1) * tile]
                    )

        def body(k, carry):
            slot = list_ref[1, k]
            a, b = slot // bcols, slot % bcols
            child(k).wait()
            blocks[a, b] = blocks[a, b] + children[k]
            return carry

        lax.fori_loop(list_ref[2, step], list_ref[2, step + 1], body, 0)

        for a in range(first, first + DEPTH):
            block_row = a * grid_rows + my_row

            @pl.when(block_row < panel_blocks)
            def _(a=a):
                blocks[a] = jnp.zeros(blocks.shape[1:], jnp.float32)

            @pl.when((my_col < panel_blocks) & (share == 0))
            def _(a=a):
                blocks[a, 0] = panel_ref[a]

            for i in range(panel_blocks):
                for j in range(panel_blocks):

                    @pl.when((block_row == i) & (my_col == j) & (share == 0))
                    def _(a=a, i=i, j=j):
                        ref = (l0_ref, None, a_ref, l1_ref)[i // 2 * 2 + j // 2]
                        if ref is None:
                            blocks[a, 0] = jnp.zeros((tile, tile), jnp.float32)
                        else:
                            part = ref.at[pl.ds(i % 2 * tile, tile), pl.ds(j % 2 * tile, tile)]
                            copy = pltpu.make_async_copy(part, blocks.at[a, 0], x_sem.at[0])
                            copy.start()
                            copy.wait()

        write(step).start()
    for step in range(steps):
        write(step).wait()


def schur_share(listed, pattern, place, before, front, got, rows, panel, corners, strips, panel_blocks):
    brows, bcols, _, tile, _ = front.shape
    width = 4 * tile
    blocks = jax.ShapeDtypeStruct((brows, bcols, tile, tile), jnp.float32)
    return pl.pallas_call(
        functools.partial(schur_kernel, panel_blocks),
        out_shape=jax.ShapeDtypeStruct(front.shape, jnp.float32),
        grid_spec=pltpu.PrefetchScalarGridSpec(
            num_scalar_prefetch=3,
            grid=(),
            in_specs=[HBM] * 3 + [WHOLE] * 3 + [ANY] * 8,
            out_specs=HBM,
            scratch_shapes=[
                pltpu.VMEM((bcols * tile, width), jnp.bfloat16),
                pltpu.VMEM((bcols * tile, width), jnp.bfloat16),
                pltpu.VMEM(blocks.shape, jnp.float32),
                pltpu.VMEM((4, bcols, tile, tile), jnp.float32),
                pltpu.VMEM(got.shape, jnp.float32),
                pltpu.SemaphoreType.DMA((got.shape[0],)),
                pltpu.SemaphoreType.DMA((brows // DEPTH,)),
                pltpu.SemaphoreType.DMA((brows // DEPTH,)),
                pltpu.SemaphoreType.DMA((4,)),
            ],
        ),
        input_output_aliases={3: 0} if before is not front else {},
        compiler_params=vmem(40, got, blocks),
        name="schur_share",
    )(listed, pattern, place, before, front, got, *rows, panel, *corners, *strips)


def in_slot_order(slots, valid):
    count = slots.shape[0]
    index = jnp.arange(count, dtype=jnp.int32)
    key = jnp.where(valid, slots, 2**20) * count + index
    place = jnp.sum((key[None, :] < key[:, None]).astype(jnp.int32), axis=1)
    at = place[None, :] == index[:, None]
    return jnp.sum(jnp.where(at, index[None, :], 0), axis=1), jnp.sum(jnp.where(at, slots[None, :], 0), axis=1)


def by_slot(slots, valid, per_step, steps):
    index = jnp.arange(slots.shape[0], dtype=jnp.int32)
    sources, ordered = in_slot_order(slots, valid)
    bound = jnp.minimum(index, steps) * per_step
    starts = jnp.sum((valid[None, :] & (slots[None, :] < bound[:, None])).astype(jnp.int32), axis=1)
    return jnp.stack([sources, ordered, starts])


def local(front, child_blocks, owners, slots, pattern):
    grid_rows = lax.axis_size("prow")
    grid_cols = lax.axis_size("pcol")
    devices = grid_rows * grid_cols
    rank_r = lax.axis_index("prow")
    rank_c = lax.axis_index("pcol")
    me = rank_r * grid_cols + rank_c
    brows, _, bcols, _, tile, _ = front.shape
    row_bits, col_bits = bits_of(grid_rows), bits_of(grid_cols)
    panel_blocks = 2 * pattern.shape[0]
    panel_bits = bits_of(panel_blocks)
    owner_ids = owners[:, 0]
    children = owner_ids.shape[0]

    notes = jnp.zeros((8, tile), jnp.float32)
    notes = notes.at[0, :children].set(owner_ids.astype(jnp.float32)).at[1, :children].set(slots.astype(jnp.float32))
    corner = front[0, 0, 0, 0]

    def spread(corner, notes, axis):
        for bit in range(panel_bits, bits_of(lax.axis_size(axis))):
            other = xor_send(jnp.concatenate([corner, notes], axis=-2), axis, bit)
            high = my_bit(axis, bit) == 1
            corner, others = jnp.where(high, other[..., : corner.shape[-2], :], corner), other[..., corner.shape[-2] :, :]
            notes = jnp.concatenate([jnp.where(high, others, notes), jnp.where(high, notes, others)], axis=-2)
        return corner, notes

    index = jnp.arange(children, dtype=jnp.int32)

    def ranked(owner):
        same = owner[..., :, None] == owner[..., None, :]
        return jnp.sum((same & (index[None, :] < index[:, None])).astype(jnp.int32), axis=-1)

    hops = list(reversed(range(1, row_bits)))
    every = gather_bits(jnp.concatenate([corner, notes], axis=0), "prow", hops)
    corner = every[(0,) * (row_bits - panel_bits)][..., :tile, :]
    notes = every[..., tile:, :].reshape(-1, tile)
    corner = jnp.concatenate([corner, jnp.broadcast_to(notes, corner.shape[:-2] + notes.shape)], axis=-2)
    packed = pack(owner_ids * CAP + ranked(owner_ids), child_blocks, devices * CAP)
    corner = gather_bit(corner, "prow", 0)
    send = after(packed, corner)
    got = lax.all_to_all(send, ALL, 0, 0, tiled=True)
    corner = after(corner, send)
    highs = grid_rows // grid_cols
    my_high = rank_r // grid_cols
    share_cols = bcols // highs
    shares = [my_high ^ high for high in range(highs)]
    ready = owner_ids[0] >= 0

    def beside_children(corner):
        corner, notes = spread(corner[..., :tile, :], corner[..., tile:, :], "pcol")
        corner = jnp.concatenate([corner, notes], axis=-2)
        corner = jnp.swapaxes(gather_bits(corner, "pcol", list(reversed(range(panel_bits)))), 0, 1)
        l0, *z0 = factor_panel0(corner)
        a, ah, al, l1, *z1 = factor_panel1(corner, pattern, z0)

        bits = row_bits + col_bits
        noted = corner[:, :, :, 0, tile:, :]
        dims = [("col", bit) for bit in range(panel_bits)] + [("row", 0)]
        dims += [("col", bit) for bit in reversed(range(panel_bits, col_bits))]
        dims += [("row", bit) for bit in reversed(range(1, row_bits))]
        noted = noted.reshape((2,) * bits + (8, tile))[..., :2, :children].astype(jnp.int32)
        linear = [("row", bit) for bit in reversed(range(row_bits))] + [("col", bit) for bit in reversed(range(col_bits))]
        every = jnp.transpose(noted, [dims.index(dim) for dim in linear] + [bits, bits + 1])
        every = every.reshape(devices, 2, children)
        every_owner, every_slot = every[:, 0], every[:, 1]
        every_rank = ranked(every_owner)
        mine = every_owner == me
        got_slots = jnp.stack(
            [jnp.sum(jnp.where(mine & (every_rank == rank), every_slot, 0), axis=1) for rank in range(CAP)], axis=1
        ).reshape(-1)
        panel_here = (got_slots > 0) & (got_slots % bcols == 0) & (rank_c < panel_blocks)
        panel_row = jnp.where(panel_here, got_slots // bcols, -1)

        def listed(share):
            inside = (got_slots > 0) & ~panel_here & (got_slots % bcols % highs == share)
            slot = got_slots // bcols * share_cols + got_slots % bcols // highs
            return by_slot(slot, inside, DEPTH * share_cols, brows // DEPTH)

        return (l0, a, l1), (*z0, ah, al, *z1), panel_row, [listed(share) for share in shares]

    corners, factors, panel_row, lists = stage(ready, beside_children, corner)
    strip = spread_high(add_to_strip(panel_row, front[:, 0, 0, 0], got), "pcol", panel_bits)

    def to_column(part, m):
        pairs = [
            ((high * grid_cols + low) * grid_cols + c, (high * grid_cols + (c ^ m)) * grid_cols + low)
            for high in range(highs)
            for low in range(grid_cols)
            for c in range(grid_cols)
        ]
        return lax.ppermute(part, ALL, [(source, target) for source, target in pairs if source != target])

    parts = {0: strip}
    for bit in reversed(range(col_bits, row_bits)):
        parts |= {key | (1 << (bit - col_bits)): xor_send(part, "prow", bit) for key, part in parts.items()}
    col_strips = [
        [to_column(parts[high], m) for m in range(panel_blocks)] + [parts[high]] for high in range(highs)
    ]
    across, beside = xor_send(strip, "pcol", 1), xor_send(strip, "pcol", 0)
    row_strips = [strip, beside, across, xor_send(across, "pcol", 0)]
    place = jnp.stack([rank_r, rank_c, jnp.int32(grid_rows)])
    row_high, row_low, panel = solve_rows(row_strips, pattern, place, factors)
    blocks = front.reshape(brows, share_cols, highs, tile, tile)
    out = blocks
    for listed, share, strips in zip(lists, shares, col_strips):
        place = jnp.stack([rank_r, rank_c, jnp.int32(grid_rows), jnp.int32(grid_cols), share])
        out = schur_share(
            listed, pattern, place, out, blocks, got, (row_high, row_low), panel, corners, strips, panel_blocks
        )
    return out.reshape(front.shape)


def solution(mesh):
    placed = (
        P(None, "prow", None, "pcol", None, None),
        P(("prow", "pcol"), None, None),
        P(("prow", "pcol"), None),
        P(("prow", "pcol")),
        P(),
    )
    return jax.shard_map(
        local,
        mesh=mesh,
        in_specs=placed,
        out_specs=P(None, "prow", None, "pcol", None, None),
        check_vma=False,
    )
```

```python
import functools

import jax
import jax.numpy as jnp
from jax import lax
from jax.experimental import pallas as pl
from jax.experimental.pallas import tpu as pltpu
from jax.sharding import PartitionSpec as P

ALL = ("prow", "pcol")
CAP = 2
DEPTH = 2
HIGHEST = lax.Precision.HIGHEST
WHOLE = pl.BlockSpec(memory_space=pltpu.VMEM)
HBM = pl.BlockSpec(memory_space=pltpu.HBM)
ANY = pl.BlockSpec(memory_space=pl.ANY)


def vmem(mib, *arrays):
    held = sum(array.size * array.dtype.itemsize for array in arrays)
    return pltpu.CompilerParams(vmem_limit_bytes=mib * 2**20 + held)


def bits_of(size):
    return size.bit_length() - 1


def xor_send(x, axis, bit):
    size = lax.axis_size(axis)
    return lax.ppermute(x, axis, [(i, i ^ (1 << bit)) for i in range(size)])


def my_bit(axis, bit):
    return (lax.axis_index(axis) >> bit) & 1


def gather_bit(x, axis, bit):
    other = xor_send(x, axis, bit)
    low = my_bit(axis, bit) == 0
    return jnp.stack([jnp.where(low, x, other), jnp.where(low, other, x)])


def gather_bits(x, bits):
    devices = lax.axis_size("prow") * lax.axis_size("pcol")
    unit = {"prow": lax.axis_size("pcol"), "pcol": 1}
    masks = [0]
    for axis, bit in bits:
        masks = [mask | on for mask in masks for on in (0, unit[axis] << bit)]
    sent = [lax.ppermute(x, ALL, [(i, i ^ mask) for i in range(devices)]) if mask else x for mask in masks]
    whole = jnp.stack(sent).reshape((2,) * len(bits) + x.shape)
    for dim, (axis, bit) in enumerate(bits):
        whole = jnp.where(my_bit(axis, bit) == 0, whole, jnp.flip(whole, dim))
    return whole


def spread_high(x, axis, low_bits):
    for bit in range(low_bits, bits_of(lax.axis_size(axis))):
        other = lax.ppermute(x, axis, [(i, i | (1 << bit)) for i in range(1 << bit)])
        x = jnp.where(my_bit(axis, bit) == 1, other, x)
    return x


def nt_dot(a, b):
    return lax.dot_general(a, b, (((1,), (1,)), ((), ())), preferred_element_type=jnp.float32)


def split(x):
    high = x.astype(jnp.bfloat16)
    return high, (x - high.astype(jnp.float32)).astype(jnp.bfloat16)


def nt_dot3(a, b):
    return nt_dot(a[0], b[0]) + (nt_dot(a[1], b[0]) + nt_dot(a[0], b[1]))


def after_kernel(x_ref, *refs):
    pass


def after(x, *others):
    return pl.pallas_call(
        after_kernel,
        out_shape=jax.ShapeDtypeStruct(x.shape, x.dtype),
        in_specs=[ANY] * (1 + len(others)),
        out_specs=ANY,
        input_output_aliases={0: 0},
        name="after",
    )(x, *others)


def stage(ready, work, *operands):
    shapes = jax.eval_shape(work, *operands)
    return lax.cond(
        ready, work, lambda *_: jax.tree.map(lambda part: jnp.zeros(part.shape, part.dtype), shapes), *operands
    )


def pack_kernel(place_ref, child_ref, out_ref, sem):
    count = child_ref.shape[0]

    def copy(k):
        return pltpu.make_async_copy(child_ref.at[k], out_ref.at[place_ref[k]], sem.at[k])

    for k in range(count):
        copy(k).start()
    for k in range(count):
        copy(k).wait()


def pack(place, child_blocks, places):
    count, tile, _ = child_blocks.shape
    return pl.pallas_call(
        pack_kernel,
        out_shape=jax.ShapeDtypeStruct((places, tile, tile), jnp.float32),
        grid_spec=pltpu.PrefetchScalarGridSpec(
            num_scalar_prefetch=1,
            grid=(),
            in_specs=[WHOLE],
            out_specs=HBM,
            scratch_shapes=[pltpu.SemaphoreType.DMA((count,))],
        ),
        compiler_params=vmem(48, child_blocks),
        name="pack_children",
    )(place, child_blocks)


def strip_kernel(row_ref, strip_ref, got_ref, out_ref, buffer, sem):
    sources = got_ref.shape[0]

    def copy(s):
        return pltpu.make_async_copy(got_ref.at[s], buffer.at[s], sem.at[s])

    for s in range(sources):
        pl.when(row_ref[s] >= 0)(lambda s=s: copy(s).start())
    out_ref[...] = strip_ref[...]
    for s in range(sources):

        @pl.when(row_ref[s] >= 0)
        def _(s=s):
            copy(s).wait()
            out_ref[row_ref[s]] = out_ref[row_ref[s]] + buffer[s]


def add_to_strip(panel_row, strip, got):
    return pl.pallas_call(
        strip_kernel,
        out_shape=jax.ShapeDtypeStruct(strip.shape, jnp.float32),
        grid_spec=pltpu.PrefetchScalarGridSpec(
            num_scalar_prefetch=1,
            grid=(),
            in_specs=[WHOLE, HBM],
            out_specs=WHOLE,
            scratch_shapes=[
                pltpu.VMEM(got.shape, jnp.float32),
                pltpu.SemaphoreType.DMA((got.shape[0],)),
            ],
        ),
        compiler_params=vmem(8, got),
        name="add_panel_children",
    )(panel_row, strip, got)


def exact_dot(a, b, dims):
    return lax.dot_general(a, b, (dims, ((), ())), precision=HIGHEST, preferred_element_type=jnp.float32)


def inverse_root(x):
    y = lax.rsqrt(x)
    return y * (1.5 - 0.5 * x * y * y)


def eliminate(work_ref, right_ref, t_ref, z_ref):
    n = work_ref.shape[0]
    row = lax.broadcasted_iota(jnp.int32, (n, n), 0)
    col = lax.broadcasted_iota(jnp.int32, (n, n), 1)
    right_ref[...] = jnp.where(row == col, 1.0, 0.0)
    for j in range(0, n, 2):
        lo = j // 8 * 8
        i = j - lo
        a = work_ref[lo:, :]
        z = right_ref[lo:, :]
        col0 = jnp.broadcast_to(a[:, j : j + 1], a.shape)
        col1 = jnp.broadcast_to(a[:, j + 1 : j + 2], a.shape)
        inv0 = inverse_root(col0[i : i + 1, :])
        row0 = a[i : i + 1, :] * inv0
        low0 = col0 * inv0
        cross = low0[i + 1 : i + 2, :]
        low1 = col1 - low0 * cross
        inv1 = inverse_root(low1[i + 1 : i + 2, :])
        row1 = (a[i + 1 : i + 2, :] - cross * row0) * inv1
        low1 = low1 * inv1
        z0 = z[i : i + 1, :] * inv0
        z1 = (z[i + 1 : i + 2, :] - cross * z0) * inv1
        if j + 2 < n:
            work_ref[lo:, :] = a - low0 * row0 - low1 * row1
            right_ref[lo:, :] = z - low0 * z0 - low1 * z1
        t_ref[j : j + 1, :] = row0
        t_ref[j + 1 : j + 2, :] = row1
        z_ref[j : j + 1, :] = z0
        z_ref[j + 1 : j + 2, :] = z1


def lower_of(t):
    n = t.shape[0]
    row = lax.broadcasted_iota(jnp.int32, (n, n), 0)
    col = lax.broadcasted_iota(jnp.int32, (n, n), 1)
    return jnp.where(col <= row, t.T, 0.0)


def symmetric(block):
    n = block.shape[0]
    row = lax.broadcasted_iota(jnp.int32, (n, n), 0)
    col = lax.broadcasted_iota(jnp.int32, (n, n), 1)
    return jnp.where(col <= row, block, block.T)


def factor_panel(g, scratch):
    work, right, t, z = scratch
    nt, nn = ((1,), (1,)), ((1,), (0,))
    work[...] = symmetric(g[0][0])
    eliminate(work, right, t, z)
    l00, z00 = lower_of(t[...]), z[...]
    l10 = exact_dot(g[1][0], z00, nt)
    work[...] = symmetric(g[1][1]) - exact_dot(l10, l10, nt)
    eliminate(work, right, t, z)
    l11, z11 = lower_of(t[...]), z[...]
    z10 = -exact_dot(z11, exact_dot(l10, z00, nn), nn)
    return (l00, l10, l11), (z00, z10, z11)


def store_square(ref, blocks):
    tile = blocks[0].shape[0]
    ref[:tile, :tile] = blocks[0]
    ref[:tile, tile:] = jnp.zeros((tile, tile), ref.dtype)
    ref[tile:, :tile] = blocks[1]
    ref[tile:, tile:] = blocks[2]


def leading_block(ref, i, j):
    return ref[j % 2, j // 2, i % 2, i // 2, : ref.shape[-1], :]


def panel0_kernel(corner_ref, l_ref, zh_ref, zl_ref, *scratch):
    g = [[leading_block(corner_ref, i, j) for j in range(2)] for i in range(2)]
    lower, inverse = factor_panel(g, scratch)
    store_square(l_ref, lower)
    parts = [split(block) for block in inverse]
    store_square(zh_ref, [part[0] for part in parts])
    store_square(zl_ref, [part[1] for part in parts])


def panel1_kernel(pattern_ref, corner_ref, z0h_ref, z0l_ref, a_ref, ah_ref, al_ref, l_ref, zh_ref, zl_ref, *scratch):
    tile = corner_ref.shape[-1]
    z0 = (z0h_ref[...], z0l_ref[...])
    rows = [jnp.concatenate([leading_block(corner_ref, 2 + i, j) for j in range(2)], axis=1) for i in range(2)]
    a = jnp.concatenate([nt_dot3(split(rows[i]), z0) * pattern_ref[0, 2 + i].astype(jnp.float32) for i in range(2)], axis=0)
    a_ref[...] = a
    ah_ref[...], al_ref[...] = split(a)
    update = exact_dot(a, a, ((1,), (1,)))
    g = [
        [leading_block(corner_ref, 2 + i, 2 + j) - update[i * tile : (i + 1) * tile, j * tile : (j + 1) * tile] for j in range(2)]
        for i in range(2)
    ]
    lower, inverse = factor_panel(g, scratch)
    store_square(l_ref, lower)
    parts = [split(block) for block in inverse]
    store_square(zh_ref, [part[0] for part in parts])
    store_square(zl_ref, [part[1] for part in parts])


def factor_panel0(corner):
    tile = corner.shape[-1]
    full = jax.ShapeDtypeStruct((2 * tile, 2 * tile), jnp.float32)
    part = jax.ShapeDtypeStruct((2 * tile, 2 * tile), jnp.bfloat16)
    return pl.pallas_call(
        panel0_kernel,
        out_shape=(full, part, part),
        in_specs=[WHOLE],
        out_specs=(WHOLE,) * 3,
        scratch_shapes=[pltpu.VMEM((tile, tile), jnp.float32)] * 4,
        compiler_params=vmem(12),
        name="factor_panel0",
    )(corner)


def factor_panel1(corner, pattern, z0):
    tile = corner.shape[-1]
    full = jax.ShapeDtypeStruct((2 * tile, 2 * tile), jnp.float32)
    part = jax.ShapeDtypeStruct((2 * tile, 2 * tile), jnp.bfloat16)
    return pl.pallas_call(
        panel1_kernel,
        out_shape=(full, part, part, full, part, part),
        grid_spec=pltpu.PrefetchScalarGridSpec(
            num_scalar_prefetch=1,
            grid=(),
            in_specs=[WHOLE] * 3,
            out_specs=(WHOLE,) * 6,
            scratch_shapes=[pltpu.VMEM((tile, tile), jnp.float32)] * 4,
        ),
        compiler_params=vmem(12),
        name="factor_panel1",
    )(pattern, corner, *z0)


def nn_dot3(a, b):
    def dot(x, y):
        return lax.dot_general(x, y, (((1,), (0,)), ((), ())), preferred_element_type=jnp.float32)

    return dot(a[0], b[0]) + (dot(a[1], b[0]) + dot(a[0], b[1]))


def rows_kernel(size, pattern_ref, place_ref, *refs):
    strip_refs, factor_refs, (high_ref, low_ref, panel_ref, xs, x_refs, sem) = refs[:4], refs[4:10], refs[10:]
    _, rows, tile, _ = x_refs.shape
    copies = [pltpu.make_async_copy(ref, x_refs.at[m], sem.at[m]) for m, ref in enumerate(strip_refs)]
    for copy in copies:
        copy.start()
    for copy in copies:
        copy.wait()
    z0, a, z1 = [(factor_refs[2 * i][...], factor_refs[2 * i + 1][...]) for i in range(3)]
    strip, base = place_ref[1] % 4, place_ref[0] % 4

    def masked(q, panel, at):
        parts = []
        for i in range(size):
            block_row = (at + i) * place_ref[2] + place_ref[0]
            keep = pattern_ref[0, block_row]
            if panel == 1:
                keep = jnp.maximum(keep, pattern_ref[1, block_row])
            parts.append(q[i * tile : (i + 1) * tile] * keep.astype(jnp.float32))
        return jnp.concatenate(parts, axis=0)

    def spread_out(first, second):
        for index, whole in enumerate((first, second)):
            xs[2 * index] = whole[:, :tile]
            xs[2 * index + 1] = whole[:, tile:]

    for at in range(0, rows, size):
        for m in range(4):
            xs[strip ^ m] = x_refs[m, at : at + size].reshape(size * tile, tile)
        x0 = jnp.concatenate([xs[0], xs[1]], axis=1)
        x1 = jnp.concatenate([xs[2], xs[3]], axis=1)
        q0 = masked(nt_dot3(split(x0), z0), 0, at)
        q0_parts = split(q0)
        q1 = masked(nt_dot3(split(x1 - nt_dot3(q0_parts, a)), z1), 1, at)
        spread_out(q0, q1)
        panel_ref[at : at + size] = xs[strip].reshape(size, tile, tile)
        w1 = nn_dot3(split(q1), z1)
        w0 = nn_dot3(split(q0 - nn_dot3(split(w1), a)), z0)
        spread_out(w0, w1)
        for m in range(4):
            high_ref[at * tile : (at + size) * tile, m * tile : (m + 1) * tile], low_ref[
                at * tile : (at + size) * tile, m * tile : (m + 1) * tile
            ] = split(xs[base ^ m])


def solve_rows(strips, pattern, place, factors):
    rows, tile, _ = strips[0].shape
    size = min(rows, 4)
    part = jax.ShapeDtypeStruct((rows * tile, 4 * tile), jnp.bfloat16)
    return pl.pallas_call(
        functools.partial(rows_kernel, size),
        out_shape=(part, part, jax.ShapeDtypeStruct((rows, tile, tile), jnp.float32)),
        grid_spec=pltpu.PrefetchScalarGridSpec(
            num_scalar_prefetch=2,
            grid=(),
            in_specs=[ANY] * 4 + [WHOLE] * 6,
            out_specs=(WHOLE,) * 3,
            scratch_shapes=[
                pltpu.VMEM((4, size * tile, tile), jnp.float32),
                pltpu.VMEM((4, rows, tile, tile), jnp.float32),
                pltpu.SemaphoreType.DMA((4,)),
            ],
        ),
        compiler_params=vmem(20),
        name="solve_rows",
    )(pattern, place, *strips, *factors)


def schur_kernel(panel_blocks, list_ref, pattern_ref, place_ref, before_ref, front_ref, got_ref, high_ref, low_ref,
                 panel_ref, l0_ref, a_ref, l1_ref, *refs):
    strip_refs, (out_ref, col_high, col_low, blocks, x_refs, children, child_sem, read_sem, write_sem, x_sem) = refs[:5], refs[5:]
    brows, bcols, tile, _ = blocks.shape
    steps = brows // DEPTH
    my_row, my_col, grid_rows, grid_cols, share = [place_ref[i] for i in range(5)]

    def child(k):
        return pltpu.make_async_copy(got_ref.at[list_ref[0, k]], children.at[k], child_sem.at[k])

    def read(step):
        rows = pl.ds(step * DEPTH, DEPTH)
        return pltpu.make_async_copy(front_ref.at[rows, :, share], blocks.at[rows], read_sem.at[step])

    def write(step):
        rows = pl.ds(step * DEPTH, DEPTH)
        return pltpu.make_async_copy(blocks.at[rows], out_ref.at[rows, :, share], write_sem.at[step])

    own = my_row % grid_cols == my_col

    def strip(m, source):
        return pltpu.make_async_copy(strip_refs[source], x_refs.at[m], x_sem.at[m])

    pl.when(own)(lambda: strip(0, 4).start())
    pl.when(jnp.logical_not(own))(lambda: strip(0, 0).start())
    for m in range(1, 4):
        strip(m, m).start()
    for step in range(steps):
        read(step).start()

    def start(k, carry):
        child(k).start()
        return carry

    lax.fori_loop(0, list_ref[2, steps], start, 0)

    for m in range(4):
        strip(m, m).wait()
        for a in range(bcols):
            block_row = a * grid_rows + share * grid_cols + my_col
            first_keep = pattern_ref[0, block_row]
            keep = jnp.where((my_row ^ m) & 2 == 0, first_keep, jnp.maximum(first_keep, pattern_ref[1, block_row]))
            high, low = split(x_refs[m, a] * keep.astype(jnp.float32))
            at = (slice(a * tile, (a + 1) * tile), slice(m * tile, (m + 1) * tile))
            col_high[at] = high
            col_low[at] = low
    for step in range(steps):
        first = step * DEPTH
        rows = tuple(ref[first * tile : (first + DEPTH) * tile, :] for ref in (high_ref, low_ref))
        read(step).wait()
        for at in range(0, bcols, 2):
            cols = slice(at * tile, (at + 2) * tile)
            update = nt_dot3(rows, (col_high[cols, :], col_low[cols, :]))
            for k in range(2):
                for a in range(DEPTH):
                    blocks[first + a, at + k] = (
                        blocks[first + a, at + k] - update[a * tile : (a + 1) * tile, k * tile : (k + 1) * tile]
                    )

        def body(k, carry):
            slot = list_ref[1, k]
            a, b = slot // bcols, slot % bcols
            child(k).wait()
            blocks[a, b] = blocks[a, b] + children[k]
            return carry

        lax.fori_loop(list_ref[2, step], list_ref[2, step + 1], body, 0)

        for a in range(first, first + DEPTH):
            block_row = a * grid_rows + my_row

            @pl.when(block_row < panel_blocks)
            def _(a=a):
                blocks[a] = jnp.zeros(blocks.shape[1:], jnp.float32)

            @pl.when((my_col < panel_blocks) & (share == 0))
            def _(a=a):
                blocks[a, 0] = panel_ref[a]

            for i in range(panel_blocks):
                for j in range(panel_blocks):

                    @pl.when((block_row == i) & (my_col == j) & (share == 0))
                    def _(a=a, i=i, j=j):
                        ref = (l0_ref, None, a_ref, l1_ref)[i // 2 * 2 + j // 2]
                        if ref is None:
                            blocks[a, 0] = jnp.zeros((tile, tile), jnp.float32)
                        else:
                            part = ref.at[pl.ds(i % 2 * tile, tile), pl.ds(j % 2 * tile, tile)]
                            copy = pltpu.make_async_copy(part, blocks.at[a, 0], x_sem.at[0])
                            copy.start()
                            copy.wait()

        write(step).start()
    for step in range(steps):
        write(step).wait()


def schur_share(listed, pattern, place, before, front, got, rows, panel, corners, strips, panel_blocks):
    brows, bcols, _, tile, _ = front.shape
    width = 4 * tile
    blocks = jax.ShapeDtypeStruct((brows, bcols, tile, tile), jnp.float32)
    return pl.pallas_call(
        functools.partial(schur_kernel, panel_blocks),
        out_shape=jax.ShapeDtypeStruct(front.shape, jnp.float32),
        grid_spec=pltpu.PrefetchScalarGridSpec(
            num_scalar_prefetch=3,
            grid=(),
            in_specs=[HBM] * 3 + [WHOLE] * 3 + [ANY] * 8,
            out_specs=HBM,
            scratch_shapes=[
                pltpu.VMEM((bcols * tile, width), jnp.bfloat16),
                pltpu.VMEM((bcols * tile, width), jnp.bfloat16),
                pltpu.VMEM(blocks.shape, jnp.float32),
                pltpu.VMEM((4, bcols, tile, tile), jnp.float32),
                pltpu.VMEM(got.shape, jnp.float32),
                pltpu.SemaphoreType.DMA((got.shape[0],)),
                pltpu.SemaphoreType.DMA((brows // DEPTH,)),
                pltpu.SemaphoreType.DMA((brows // DEPTH,)),
                pltpu.SemaphoreType.DMA((4,)),
            ],
        ),
        input_output_aliases={3: 0} if before is not front else {},
        compiler_params=vmem(40, got, blocks),
        name="schur_share",
    )(listed, pattern, place, before, front, got, *rows, panel, *corners, *strips)


def in_slot_order(slots, valid):
    count = slots.shape[0]
    index = jnp.arange(count, dtype=jnp.int32)
    key = jnp.where(valid, slots, 2**20) * count + index
    place = jnp.sum((key[None, :] < key[:, None]).astype(jnp.int32), axis=1)
    at = place[None, :] == index[:, None]
    return jnp.sum(jnp.where(at, index[None, :], 0), axis=1), jnp.sum(jnp.where(at, slots[None, :], 0), axis=1)


def by_slot(slots, valid, per_step, steps):
    index = jnp.arange(slots.shape[0], dtype=jnp.int32)
    sources, ordered = in_slot_order(slots, valid)
    bound = jnp.minimum(index, steps) * per_step
    starts = jnp.sum((valid[None, :] & (slots[None, :] < bound[:, None])).astype(jnp.int32), axis=1)
    return jnp.stack([sources, ordered, starts])


def local(front, child_blocks, owners, slots, pattern):
    grid_rows = lax.axis_size("prow")
    grid_cols = lax.axis_size("pcol")
    devices = grid_rows * grid_cols
    rank_r = lax.axis_index("prow")
    rank_c = lax.axis_index("pcol")
    me = rank_r * grid_cols + rank_c
    brows, _, bcols, _, tile, _ = front.shape
    row_bits, col_bits = bits_of(grid_rows), bits_of(grid_cols)
    panel_blocks = 2 * pattern.shape[0]
    panel_bits = bits_of(panel_blocks)
    owner_ids = owners[:, 0]
    children = owner_ids.shape[0]

    notes = jnp.zeros((8, tile), jnp.float32)
    notes = notes.at[0, :children].set(owner_ids.astype(jnp.float32)).at[1, :children].set(slots.astype(jnp.float32))
    corner = front[0, 0, 0, 0]

    def spread(corner, notes, axis):
        for bit in range(panel_bits, bits_of(lax.axis_size(axis))):
            other = xor_send(jnp.concatenate([corner, notes], axis=-2), axis, bit)
            high = my_bit(axis, bit) == 1
            corner, others = jnp.where(high, other[..., : corner.shape[-2], :], corner), other[..., corner.shape[-2] :, :]
            notes = jnp.concatenate([jnp.where(high, others, notes), jnp.where(high, notes, others)], axis=-2)
        return corner, notes

    index = jnp.arange(children, dtype=jnp.int32)

    def ranked(owner):
        same = owner[..., :, None] == owner[..., None, :]
        return jnp.sum((same & (index[None, :] < index[:, None])).astype(jnp.int32), axis=-1)

    hops = [("prow", bit) for bit in reversed(range(1, row_bits))]
    every = gather_bits(jnp.concatenate([corner, notes], axis=0), hops)
    corner = every[(0,) * (row_bits - panel_bits)][..., :tile, :]
    notes = every[..., tile:, :].reshape(-1, tile)
    corner = jnp.concatenate([corner, jnp.broadcast_to(notes, corner.shape[:-2] + notes.shape)], axis=-2)
    packed = pack(owner_ids * CAP + ranked(owner_ids), child_blocks, devices * CAP)
    send = after(packed, corner)
    got = lax.all_to_all(send, ALL, 0, 0, tiled=True)
    corner = after(corner, send)
    highs = grid_rows // grid_cols
    my_high = rank_r // grid_cols
    share_cols = bcols // highs
    shares = [my_high ^ high for high in range(highs)]
    ready = owner_ids[0] >= 0

    def beside_children(corner):
        corner, notes = spread(corner[..., :tile, :], corner[..., tile:, :], "pcol")
        corner = jnp.concatenate([corner, notes], axis=-2)
        corner = gather_bits(corner, [("pcol", bit) for bit in range(1, panel_bits)] + [("prow", 0)])
        corner = gather_bit(corner, "pcol", 0)
        l0, *z0 = factor_panel0(corner)
        a, ah, al, l1, *z1 = factor_panel1(corner, pattern, z0)

        bits = row_bits + col_bits
        noted = corner[:, :, :, 0, tile:, :]
        dims = [("col", bit) for bit in range(panel_bits)] + [("row", 0)]
        dims += [("col", bit) for bit in reversed(range(panel_bits, col_bits))]
        dims += [("row", bit) for bit in reversed(range(1, row_bits))]
        noted = noted.reshape((2,) * bits + (8, tile))[..., :2, :children].astype(jnp.int32)
        linear = [("row", bit) for bit in reversed(range(row_bits))] + [("col", bit) for bit in reversed(range(col_bits))]
        every = jnp.transpose(noted, [dims.index(dim) for dim in linear] + [bits, bits + 1])
        every = every.reshape(devices, 2, children)
        every_owner, every_slot = every[:, 0], every[:, 1]
        every_rank = ranked(every_owner)
        mine = every_owner == me
        got_slots = jnp.stack(
            [jnp.sum(jnp.where(mine & (every_rank == rank), every_slot, 0), axis=1) for rank in range(CAP)], axis=1
        ).reshape(-1)
        panel_here = (got_slots > 0) & (got_slots % bcols == 0) & (rank_c < panel_blocks)
        panel_row = jnp.where(panel_here, got_slots // bcols, -1)

        def listed(share):
            inside = (got_slots > 0) & ~panel_here & (got_slots % bcols % highs == share)
            slot = got_slots // bcols * share_cols + got_slots % bcols // highs
            return by_slot(slot, inside, DEPTH * share_cols, brows // DEPTH)

        return (l0, a, l1), (*z0, ah, al, *z1), panel_row, [listed(share) for share in shares]

    corners, factors, panel_row, lists = stage(ready, beside_children, corner)
    strip = spread_high(add_to_strip(panel_row, front[:, 0, 0, 0], got), "pcol", panel_bits)

    def to_column(part, m):
        pairs = [
            ((high * grid_cols + low) * grid_cols + c, (high * grid_cols + (c ^ m)) * grid_cols + low)
            for high in range(highs)
            for low in range(grid_cols)
            for c in range(grid_cols)
        ]
        return lax.ppermute(part, ALL, [(source, target) for source, target in pairs if source != target])

    parts = {0: strip}
    for bit in reversed(range(col_bits, row_bits)):
        parts |= {key | (1 << (bit - col_bits)): xor_send(part, "prow", bit) for key, part in parts.items()}
    col_strips = [
        [to_column(parts[high], m) for m in range(panel_blocks)] + [parts[high]] for high in range(highs)
    ]
    across, beside = xor_send(strip, "pcol", 1), xor_send(strip, "pcol", 0)
    row_strips = [strip, beside, across, xor_send(across, "pcol", 0)]
    place = jnp.stack([rank_r, rank_c, jnp.int32(grid_rows)])
    row_high, row_low, panel = solve_rows(row_strips, pattern, place, factors)
    blocks = front.reshape(brows, share_cols, highs, tile, tile)
    out = blocks
    for listed, share, strips in zip(lists, shares, col_strips):
        place = jnp.stack([rank_r, rank_c, jnp.int32(grid_rows), jnp.int32(grid_cols), share])
        out = schur_share(
            listed, pattern, place, out, blocks, got, (row_high, row_low), panel, corners, strips, panel_blocks
        )
    return out.reshape(front.shape)


def solution(mesh):
    placed = (
        P(None, "prow", None, "pcol", None, None),
        P(("prow", "pcol"), None, None),
        P(("prow", "pcol"), None),
        P(("prow", "pcol")),
        P(),
    )
    return jax.shard_map(
        local,
        mesh=mesh,
        in_specs=placed,
        out_specs=P(None, "prow", None, "pcol", None, None),
        check_vma=False,
    )
```
